32 devices in a mesh: section: 4 (over z), tensor: 2 (over x), dp: 4 (over y, core).
Axes of the slice: x: 2, y: 2, z: 4, core: 2. Of those that a mesh axis runs over, the one named last changes fastest.
Arguments:
- hidden_in: bfloat16 [8, 64, 4096], P('dp', None, 'tensor'), may hold values from -6 to 6
- lengths: int32 [8], P('dp'), may hold values from 16 to 64
- gains: bfloat16 [4, 4096], P('section', 'tensor'), may hold values from 0.25 to 1.75
- w_query: bfloat16 [4, 4096, 4096], P('section', None, 'tensor'), may hold values from -0.09375 to 0.09375
- w_keyval: bfloat16 [4, 4096, 8, 256], P('section', None, 'tensor'), may hold values from -0.09375 to 0.09375
- w_out: bfloat16 [4, 4096, 4096], P('section', 'tensor'), may hold values from -0.09375 to 0.09375
- grad_out: bfloat16 [8, 64, 4096], P('dp', None, 'tensor'), may hold values from -6 to 6
Outputs:
- grad_query: float32 [4, 4096, 4096], P('section', 'dp', 'tensor')
- grad_keyval: float32 [4, 4096, 8, 256], P('section', 'dp', 'tensor')
- grad_outproj: float32 [4, 4096, 4096], P('section', 'tensor', 'dp')
- grad_gain: float32 [4, 4096], P('section', ('tensor', 'dp'))
The draws below stay inside these ranges and needn't reach their ends.
Inputs may be any that keep to these rules, and one draw needn't show every extreme that they name: `lengths`: A row's keys at positions at or beyond its length are padding.
All inputs are finite; a program needn't handle non-finite values.
Results may differ from the reference program's by a relative error of at most 0.035.
Values may be sent and summed in bfloat16 or wider, within the bound.
A program may use at most 256 MiB of HBM per device.

```python
import jax
import jax.numpy as jnp
from jax import lax

D = 4096
HEADS = 32
KV_HEADS = 8
HEAD_DIM = 128
LEN = 64
MICRO = 2
BATCH = 8
N_SECTION = 4
N_DP = 4


def touch_ends(array, own_key, smallest, top_value):
    longest = array.shape.index(max(array.shape))
    spots = []
    for shift in (0, 1):
        where = [jax.random.randint(jax.random.fold_in(own_key, axis), (), 0, length) for axis, length in enumerate(array.shape)]
        where[longest] = (where[longest] + shift) % array.shape[longest]
        spots.append(tuple(where))
    return array.at[spots[0]].set(smallest).at[spots[1]].set(top_value)


def block_levels(rng, extent, cuts, least, high):
    def one(axis_at, shards_of):
        heights = jax.random.uniform(jax.random.fold_in(jax.random.fold_in(rng, 6), axis_at), (shards_of,), jnp.float32, least / len(cuts), high / len(cuts))
        return jnp.repeat(jnp.exp(heights), extent[axis_at] // shards_of).reshape((-1,) + (1,) * (len(extent) - axis_at - 1))

    gain = one(*cuts[0])
    for cut in cuts[1:]:
        gain = gain * one(*cut)
    return gain


def normal_values(key, extent, deviation, bound, cuts=(), dtype=jnp.bfloat16):
    gain = block_levels(key, extent, cuts, -0.22, 0.18) if cuts else 1.0
    values = jax.random.normal(key, extent, jnp.float32) * deviation * gain
    return jnp.minimum(jnp.maximum(values, -bound), bound).astype(dtype)


def setup_inputs(seed: int = 0) -> dict:
    key_list = jax.random.split(jax.random.key(seed), 8)
    hidden_in = normal_values(key_list[0], (BATCH, LEN, D), 1.0, 6.0, ((0, 4), (2, 2)))
    lengths = touch_ends(jax.random.randint(key_list[1], (BATCH,), LEN // 4, LEN + 1), jax.random.fold_in(key_list[1], 1), LEN // 4, LEN).astype(jnp.int32)
    gains = jnp.clip(1.0 + 0.15 * jax.random.normal(key_list[2], (N_SECTION, D), jnp.float32), 0.25, 1.75).astype(jnp.bfloat16)
    w_query = normal_values(key_list[3], (N_SECTION, D, HEADS * HEAD_DIM), D ** -0.5, 0.09375, ((0, 4), (2, 2)))
    w_keyval = normal_values(key_list[4], (N_SECTION, D, KV_HEADS, 2 * HEAD_DIM), D ** -0.5, 0.09375, ((0, 4), (2, 2)))
    w_out = normal_values(key_list[5], (N_SECTION, HEADS * HEAD_DIM, D), (HEADS * HEAD_DIM) ** -0.5, 0.09375, ((0, 4), (1, 2)))
    grad_out = normal_values(key_list[6], (BATCH, LEN, D), 1.0, 6.0, ((0, 4), (2, 2)))
    return {"hidden_in": hidden_in, "lengths": lengths, "gains": gains, "w_query": w_query, "w_keyval": w_keyval, "w_out": w_out, "grad_out": grad_out}


EPS = 1e-05
NEG = -1e+30

def settle(operand):
    return lax.optimization_barrier(operand.astype(jnp.bfloat16)).astype(jnp.float32)

def attend(queries, keyval, length):
    row_count = queries.shape[0]
    group_size = HEADS // KV_HEADS
    query_heads = queries.astype(jnp.float32).reshape(row_count, KV_HEADS, group_size, HEAD_DIM)
    pairs = keyval.astype(jnp.float32).reshape(row_count, KV_HEADS, 2, HEAD_DIM)
    scores = jnp.einsum('ighd,jgd->ghij', query_heads, pairs[:, :, 0]) * HEAD_DIM ** (-0.5)
    position = jnp.arange(row_count)
    allowed = (position[None, :] <= position[:, None]) & (position[None, :] < length)
    scores = jnp.where(allowed, scores, NEG)
    highest = lax.optimization_barrier(jnp.max(scores, -1, keepdims=True))
    raised = jnp.exp(scores - highest)
    attn_weights = raised / lax.optimization_barrier(jnp.sum(raised, -1, keepdims=True))
    head_mix = jnp.einsum('ghij,jgd->ighd', settle(attn_weights), pairs[:, :, 1])
    return (head_mix.reshape(row_count, -1).astype(jnp.bfloat16), attn_weights)

def attend_back(queries, keyval, attn_weights, mix_grad):
    row_count = queries.shape[0]
    group_size = HEADS // KV_HEADS
    query_heads = queries.astype(jnp.float32).reshape(row_count, KV_HEADS, group_size, HEAD_DIM)
    pairs = keyval.astype(jnp.float32).reshape(row_count, KV_HEADS, 2, HEAD_DIM)
    grad_heads = mix_grad.astype(jnp.float32).reshape(row_count, KV_HEADS, group_size, HEAD_DIM)
    value_grad = jnp.einsum('ghij,ighd->jgd', settle(attn_weights), grad_heads).astype(jnp.bfloat16)
    weight_grad = jnp.einsum('ighd,jgd->ghij', grad_heads, pairs[:, :, 1])
    score_grad = attn_weights * (weight_grad - lax.optimization_barrier(jnp.sum(weight_grad * attn_weights, -1, keepdims=True))) * HEAD_DIM ** (-0.5)
    score_grad = settle(score_grad)
    query_grad = jnp.einsum('ghij,jgd->ighd', score_grad, pairs[:, :, 0]).reshape(row_count, -1).astype(jnp.bfloat16)
    key_grad = jnp.einsum('ghij,ighd->jgd', score_grad, query_heads).astype(jnp.bfloat16)
    return (query_grad, jnp.stack([key_grad, value_grad], 2).reshape(row_count, -1))

def layer_forward(current, length, gain_row, query_weight, pair_weight, out_weight):
    current_wide = current.astype(jnp.float32)
    scale_row = lax.rsqrt(lax.optimization_barrier(jnp.sum(current_wide * current_wide, -1)) / D + EPS)
    normed = (current_wide * scale_row[:, None] * gain_row).astype(jnp.bfloat16)
    queries = jnp.dot(normed, query_weight, preferred_element_type=jnp.float32).astype(jnp.bfloat16)
    keyval = jnp.dot(normed, pair_weight, preferred_element_type=jnp.float32).astype(jnp.bfloat16)
    head_mix, attn_weights = attend(queries, keyval, length)
    result = (current_wide + jnp.dot(head_mix, out_weight, preferred_element_type=jnp.float32)).astype(jnp.bfloat16)
    return (result, (scale_row, normed, queries, keyval, head_mix, attn_weights))

def layer_backward(current, gain_row, query_weight, pair_weight, out_weight, kept, out_grad):
    scale_row, normed, queries, keyval, head_mix, attn_weights = kept
    mix_grad = jnp.dot(out_grad, out_weight.T, preferred_element_type=jnp.float32).astype(jnp.bfloat16)
    out_term = jnp.dot(head_mix.T, out_grad, preferred_element_type=jnp.float32)
    query_grad, pair_grad = attend_back(queries, keyval, attn_weights, mix_grad)
    query_term = jnp.dot(normed.T, query_grad, preferred_element_type=jnp.float32)
    pair_term = jnp.dot(normed.T, pair_grad, preferred_element_type=jnp.float32)
    normed_grad = jnp.dot(query_grad, query_weight.T, preferred_element_type=jnp.float32) + jnp.dot(pair_grad, pair_weight.T, preferred_element_type=jnp.float32)
    current_wide = current.astype(jnp.float32)
    gain_term = lax.optimization_barrier(jnp.sum(normed_grad * current_wide * scale_row[:, None], 0))
    correction = lax.optimization_barrier(jnp.sum(normed_grad * gain_row * current_wide, -1))
    input_grad = (out_grad.astype(jnp.float32) + scale_row[:, None] * gain_row * normed_grad - current_wide * (scale_row ** 3 / D)[:, None] * correction[:, None]).astype(jnp.bfloat16)
    return (input_grad, (query_term, pair_term, out_term, gain_term))

def reference(hidden_in, lengths, gains, w_query, w_keyval, w_out, grad_out):
    pair_weights = w_keyval.reshape(N_SECTION, D, -1)
    rows_all = hidden_in.reshape(N_DP, MICRO, LEN, D)
    lens_all = lengths.reshape(N_DP, MICRO)
    cots_all = grad_out.reshape(N_DP, MICRO, LEN, D)
    shapes = [(D, HEADS * HEAD_DIM), (D, KV_HEADS * 2 * HEAD_DIM), (HEADS * HEAD_DIM, D), (D,)]

    def replica(totals, replica_item):
        rows_here, lens_here, cots_here = replica_item
        section_sums = [tuple((jnp.zeros(shape_one, jnp.float32) for shape_one in shapes)) for section in range(N_SECTION)]
        for batch_row in range(MICRO):
            current = rows_here[batch_row]
            length = lens_here[batch_row]
            inputs = []
            kept_all = []
            for section in range(N_SECTION):
                inputs.append(current)
                current, kept = layer_forward(current, length, gains[section], w_query[section], pair_weights[section], w_out[section])
                kept_all.append(kept)
            out_grad = cots_here[batch_row]
            for section in reversed(range(N_SECTION)):
                out_grad, terms = layer_backward(inputs[section], gains[section], w_query[section], pair_weights[section], w_out[section], kept_all[section], out_grad)
                section_sums[section] = tuple((former + latter for former, latter in zip(section_sums[section], terms)))
        new_totals = tuple((total + jnp.stack([section_sums[section][member] for section in range(N_SECTION)]) for member, total in enumerate(totals)))
        return (new_totals, None)
    start = tuple((jnp.zeros((N_SECTION,) + shape_one, jnp.float32) for shape_one in shapes))
    totals, unused = lax.scan(replica, start, (rows_all, lens_all, cots_all))
    return (totals[0], totals[1].reshape(N_SECTION, D, KV_HEADS, 2 * HEAD_DIM), totals[2], totals[3])
```

```python
import jax
import jax.numpy as jnp
from jax import lax
from jax.sharding import PartitionSpec as P

HEAD_DIM = 128


EPS = 1e-05
NEG = -1e30


def shifted(block, axis, distance):
    devices = range(lax.axis_size(axis))
    route = [(i - distance, i) for i in devices if i - distance in devices]
    return lax.ppermute(block, axis, route)


def features(operand):
    return lax.all_gather(operand, "tensor", axis=1, tiled=True)


def head_total(operand):
    ranks = lax.axis_size("tensor")
    rank = lax.axis_index("tensor")
    width = operand.shape[1] // ranks
    total = lax.dynamic_slice_in_dim(operand, rank * width, width, 1)
    for distance in range(1, ranks):
        target = lax.rem(rank + distance, ranks)
        block = lax.dynamic_slice_in_dim(operand, target * width, width, 1).astype(jnp.bfloat16)
        route = [(i, (i + distance) % ranks) for i in range(ranks)]
        total = total + lax.ppermute(block, "tensor", route).astype(jnp.float32)
    return total


def replica_bits():
    ranks = lax.axis_size("dp")
    return [1 << power for power in reversed(range(ranks.bit_length() - 1))]


def exchange(block, mask):
    return lax.ppermute(block, "dp", [(i, i ^ mask) for i in range(lax.axis_size("dp"))])


def every_row(block):
    for bit in replica_bits():
        block = jnp.concatenate([block, exchange(block, bit)], 0)
    return block


def own_columns(block):
    ranks = lax.axis_size("dp")
    rank = lax.axis_index("dp")
    width = block.shape[1] // ranks
    masks = [0]
    for bit in replica_bits():
        masks = masks + [mask ^ bit for mask in masks]
    pieces = []
    for mask in masks:
        target = jnp.bitwise_xor(rank, mask)
        piece = lax.dynamic_slice_in_dim(block, target * width, width, 1)
        pieces.append(exchange(piece, mask) if mask else piece)
    return jnp.concatenate(pieces, 0)


def neighbour(operand, offset):
    return shifted(operand, "section", offset)


def inner(former, latter):
    return lax.dot_general(
        former, latter, (((0,), (0,)), ((), ())), preferred_element_type=jnp.float32
    )


def outer_side(former, latter):
    return lax.dot_general(
        former, latter, (((1,), (1,)), ((), ())), preferred_element_type=jnp.float32
    )


def select_step(stacked, position):
    return lax.dynamic_index_in_dim(stacked, position, 0, keepdims=False)


def attend(queries, keyval, length):
    row_count = queries.shape[0]
    pair_count = keyval.shape[1] // (2 * HEAD_DIM)
    group_size = queries.shape[1] // (HEAD_DIM * pair_count)
    query_heads = queries.reshape(row_count, pair_count, group_size, HEAD_DIM)
    pairs = keyval.reshape(row_count, pair_count, 2, HEAD_DIM)
    scores = jnp.einsum(
        "ighd,jgd->ghij", query_heads, pairs[:, :, 0], preferred_element_type=jnp.float32
    ) * HEAD_DIM ** (-0.5)
    position = jnp.arange(row_count)
    allowed = (position[None, :] <= position[:, None]) & (position[None, :] < length)
    scores = jnp.where(allowed, scores, NEG)
    highest = jnp.max(scores, -1, keepdims=True)
    raised = jnp.exp(scores - highest)
    attn_weights = raised / jnp.sum(raised, -1, keepdims=True)
    head_mix = jnp.einsum(
        "ghij,jgd->ighd",
        attn_weights.astype(jnp.bfloat16),
        pairs[:, :, 1],
        preferred_element_type=jnp.float32,
    )
    return (head_mix.reshape(row_count, -1).astype(jnp.bfloat16), attn_weights)


def attend_back(queries, keyval, attn_weights, mix_grad):
    row_count = queries.shape[0]
    pair_count = keyval.shape[1] // (2 * HEAD_DIM)
    group_size = queries.shape[1] // (HEAD_DIM * pair_count)
    query_heads = queries.reshape(row_count, pair_count, group_size, HEAD_DIM)
    pairs = keyval.reshape(row_count, pair_count, 2, HEAD_DIM)
    grad_heads = mix_grad.reshape(row_count, pair_count, group_size, HEAD_DIM)
    value_grad = jnp.einsum(
        "ghij,ighd->jgd",
        attn_weights.astype(jnp.bfloat16),
        grad_heads,
        preferred_element_type=jnp.float32,
    ).astype(jnp.bfloat16)
    weight_grad = jnp.einsum(
        "ighd,jgd->ghij", grad_heads, pairs[:, :, 1], preferred_element_type=jnp.float32
    )
    score_grad = (
        attn_weights
        * (weight_grad - jnp.sum(weight_grad * attn_weights, -1, keepdims=True))
        * HEAD_DIM ** (-0.5)
    )
    score_grad = score_grad.astype(jnp.bfloat16)
    query_grad = (
        jnp.einsum("ghij,jgd->ighd", score_grad, pairs[:, :, 0], preferred_element_type=jnp.float32)
        .reshape(row_count, -1)
        .astype(jnp.bfloat16)
    )
    key_grad = jnp.einsum(
        "ghij,ighd->jgd", score_grad, query_heads, preferred_element_type=jnp.float32
    ).astype(jnp.bfloat16)
    return (query_grad, jnp.stack([key_grad, value_grad], 2).reshape(row_count, -1))


def window_rows(stacked, first_step, micro_count):
    picked = lax.dynamic_slice_in_dim(stacked, first_step, micro_count, 0)
    return picked.reshape(micro_count * picked.shape[1], picked.shape[2])


def shards(hidden_in, lengths, gains, w_query, w_keyval, w_out, grad_out):
    sections = lax.axis_size("section")
    station = lax.axis_index("section")
    micro_count = hidden_in.shape[0]
    step_count = micro_count + sections - 1
    gain_row = gains[0]
    gain_full = features(gains)[0].astype(jnp.float32)
    query_weight = w_query[0]
    model_width = query_weight.shape[0]
    pair_count = w_keyval.shape[2]
    pair_weight = w_keyval[0].reshape(model_width, -1)
    out_weight = w_out[0]
    incoming = jnp.zeros_like(hidden_in[0])
    kept_items = []
    for moment in range(step_count):
        slot_index = jnp.clip(moment - station, 0, micro_count - 1)
        own_rows = lax.dynamic_index_in_dim(hidden_in, slot_index, 0, keepdims=False)
        current = jnp.where(station == 0, own_rows, incoming)
        length = lax.dynamic_index_in_dim(lengths, slot_index, 0, keepdims=False)
        current_wide = current.astype(jnp.float32)
        current_full = features(current)
        full_wide = current_full.astype(jnp.float32)
        scale_row = lax.rsqrt(jnp.sum(full_wide * full_wide, -1) / model_width + EPS)
        normed = (full_wide * scale_row[:, None] * gain_full).astype(jnp.bfloat16)
        queries = jnp.dot(normed, query_weight, preferred_element_type=jnp.float32).astype(
            jnp.bfloat16
        )
        keyval = jnp.dot(normed, pair_weight, preferred_element_type=jnp.float32).astype(
            jnp.bfloat16
        )
        head_mix, attn_weights = attend(queries, keyval, length)
        branch = head_total(jnp.dot(head_mix, out_weight, preferred_element_type=jnp.float32))
        result = (current_wide + branch).astype(jnp.bfloat16)
        kept_items.append((current, current_full, scale_row, normed, queries, keyval, head_mix, attn_weights))
        if moment + 1 < step_count:
            incoming = neighbour(result, 1)
    past_input, past_full, past_scale, past_normed, past_queries, past_keyval, past_mix, past_weights = [
        jnp.stack(list(member_items)) for member_items in zip(*kept_items)
    ]
    normed_rows = own_columns(window_rows(past_normed, station, micro_count))
    mixed_rows = every_row(window_rows(past_mix, station, micro_count))
    incoming_grad = jnp.zeros_like(grad_out[0])
    gain_grad = jnp.zeros(gain_row.shape, jnp.float32)
    collected = []
    for moment in range(step_count):
        batch_offset = moment - (sections - 1 - station)
        is_valid = (batch_offset >= 0) & (batch_offset < micro_count)
        slot_index = jnp.clip(batch_offset, 0, micro_count - 1)
        forward_step = jnp.clip(batch_offset + station, 0, step_count - 1)
        own_grad = lax.dynamic_index_in_dim(grad_out, slot_index, 0, keepdims=False)
        current_grad = jnp.where(station == sections - 1, own_grad, incoming_grad)
        current = select_step(past_input, forward_step)
        scale_row = select_step(past_scale, forward_step)
        current_full = select_step(past_full, forward_step).astype(jnp.float32)
        queries = select_step(past_queries, forward_step)
        keyval = select_step(past_keyval, forward_step)
        attn_weights = select_step(past_weights, forward_step)
        full_grad = features(current_grad)
        mix_grad = outer_side(full_grad, out_weight).astype(jnp.bfloat16)
        query_grad, pair_grad = attend_back(queries, keyval, attn_weights, mix_grad)
        partial_grad = outer_side(query_grad, query_weight) + outer_side(pair_grad, pair_weight)
        correction = lax.psum(jnp.sum(partial_grad * gain_full * current_full, -1), "tensor")
        normed_grad = head_total(partial_grad)
        current_wide = current.astype(jnp.float32)
        gain_step = jnp.sum(normed_grad * current_wide * scale_row[:, None], 0)
        gain_grad = gain_grad + jnp.where(is_valid, gain_step, 0.0)
        input_grad = (
            current_grad.astype(jnp.float32)
            + scale_row[:, None] * gain_row * normed_grad
            - current_wide * (scale_row**3 / model_width)[:, None] * correction[:, None]
        ).astype(jnp.bfloat16)
        collected.append((jnp.concatenate([query_grad, pair_grad], 1), full_grad))
        if moment + 1 < step_count:
            incoming_grad = neighbour(input_grad, -1)
    first_step = sections - 1 - station
    pair_rows, outgrad_rows = [
        window_rows(jnp.stack(list(member_items)), first_step, micro_count)
        for member_items in zip(*collected)
    ]
    output_total = inner(mixed_rows, own_columns(outgrad_rows))
    pair_rows = every_row(pair_rows)
    query_width = query_weight.shape[1]
    query_total = inner(normed_rows, pair_rows[:, :query_width])
    pair_total = inner(normed_rows, pair_rows[:, query_width:])
    gain_total = lax.psum_scatter(gain_grad, "dp", scatter_dimension=0, tiled=True)
    grad_query = query_total[None]
    grad_keyval = pair_total.reshape(1, pair_total.shape[0], pair_count, 2 * HEAD_DIM)
    grad_outproj = output_total[None]
    grad_gain = gain_total[None]
    return (grad_query, grad_keyval, grad_outproj, grad_gain)


def solution(mesh):
    in_specs = (
        P("dp", None, "tensor"),
        P("dp"),
        P("section", "tensor"),
        P("section", None, "tensor"),
        P("section", None, "tensor", None),
        P("section", "tensor", None),
        P("dp", None, "tensor"),
    )
    out_specs = (
        P("section", "dp", "tensor"),
        P("section", "dp", "tensor", None),
        P("section", "tensor", "dp"),
        P("section", ("tensor", "dp")),
    )
    return jax.shard_map(shards, mesh=mesh, in_specs=in_specs, out_specs=out_specs, check_vma=False)
```

```python
import functools

import jax
import jax.numpy as jnp
from jax import lax
from jax.experimental import pallas as pl
from jax.experimental.pallas import tpu as pltpu
from jax.sharding import PartitionSpec as P

HEAD_DIM = 128


EPS = 1e-05
NEG = -1e30


def inner(former, latter):
    return lax.dot_general(
        former, latter, (((0,), (0,)), ((), ())), preferred_element_type=jnp.float32
    )


def outer_side(former, latter):
    return lax.dot_general(
        former, latter, (((1,), (1,)), ((), ())), preferred_element_type=jnp.float32
    )


def plain(former, latter):
    return jnp.dot(former, latter, preferred_element_type=jnp.float32)


def replica_bits():
    ranks = lax.axis_size("dp")
    return [1 << power for power in reversed(range(ranks.bit_length() - 1))]


def exchange(block, mask):
    return lax.ppermute(block, "dp", [(i, i ^ mask) for i in range(lax.axis_size("dp"))])


def every_row(block):
    for bit in replica_bits():
        block = jnp.concatenate([block, exchange(block, bit)], 0)
    return block


def own_columns(block):
    ranks = lax.axis_size("dp")
    rank = lax.axis_index("dp")
    width = block.shape[1] // ranks
    masks = [0]
    for bit in replica_bits():
        masks = masks + [mask ^ bit for mask in masks]
    pieces = []
    for mask in masks:
        target = jnp.bitwise_xor(rank, mask)
        piece = lax.dynamic_slice_in_dim(block, target * width, width, 1)
        pieces.append(exchange(piece, mask) if mask else piece)
    return jnp.concatenate(pieces, 0)


def tile_of(width):
    return 512 if width % 512 == 0 else 256


def tiles(width, body):
    size = tile_of(width)

    def step(index, carry):
        body(pl.multiple_of(index * size, size), size)
        return carry

    lax.fori_loop(0, width // size, step, 0)


def kernel(
    ranks, sections, micro,
    hidden, mask, gains, wq_hbm, wkv_hbm, wo_hbm, grad_out,
    normed, mixed, pair_rows, grad_rows, gain_grad,
    wq, wkv, wo, hfull, gfull, gain_all, scales, queries, keyval, weights, mix_grad,
    own, send_f, recv_f, send_b, recv_b, next_h, next_g, corr_out, corr_in,
    load_sem, gain_sem, ag_sem, rs_sem, z_sem, corr_sem,
):
    rank = lax.axis_index("tensor")
    station = lax.axis_index("section")
    rows = hidden.shape[1]
    width = hidden.shape[2]
    model = ranks * width
    q_width = wq.shape[1]
    pairs = wkv.shape[1] // (2 * HEAD_DIM)
    group = q_width // (HEAD_DIM * pairs)
    first, last = station == 0, station == sections - 1

    def peer(distance):
        return lax.rem(rank + distance, ranks)

    def remote(source, target, sems, device):
        return pltpu.make_async_remote_copy(
            src_ref=source, dst_ref=target, send_sem=sems[0], recv_sem=sems[1],
            device_id=device, device_id_type=pl.DeviceIdType.MESH,
        )

    barrier = pltpu.get_barrier_semaphore()
    for distance in range(1, ranks):
        pl.semaphore_signal(
            barrier, inc=1, device_id={"tensor": peer(distance)},
            device_id_type=pl.DeviceIdType.MESH,
        )

    @pl.when(station > 0)
    def _():
        pl.semaphore_signal(
            barrier, inc=1, device_id={"section": station - 1},
            device_id_type=pl.DeviceIdType.MESH,
        )

    @pl.when(station < sections - 1)
    def _():
        pl.semaphore_signal(
            barrier, inc=1, device_id={"section": station + 1},
            device_id_type=pl.DeviceIdType.MESH,
        )

    loads = [
        pltpu.make_async_copy(source, target, load_sem.at[index])
        for index, (source, target) in enumerate(((wq_hbm, wq), (wkv_hbm, wkv), (wo_hbm, wo)))
    ]
    for load in loads:
        load.start()

    ends = jnp.where(first, 0, 1) + jnp.where(last, 0, 1)
    pl.semaphore_wait(barrier, ranks - 1 + ends)

    def gain_copy(distance):
        return remote(
            gain_all.at[rank], gain_all.at[rank],
            (gain_sem.at[0, distance - 1], gain_sem.at[1, distance - 1]),
            {"tensor": peer(distance)},
        )

    def gather_copy(way, m, distance):
        full = (hfull, gfull)[way]
        return remote(
            full.at[m, rank], full.at[m, rank],
            (ag_sem.at[way, 0, m, distance - 1], ag_sem.at[way, 1, m, distance - 1]),
            {"tensor": peer(distance)},
        )

    def sum_copy(way, m, distance):
        return remote(
            (send_f, send_b)[way].at[m, distance - 1], (recv_f, recv_b)[way].at[m, distance - 1],
            (rs_sem.at[way, 0, m, distance - 1], rs_sem.at[way, 1, m, distance - 1]),
            {"tensor": peer(distance)},
        )

    def corr_copy(m, distance):
        return remote(
            corr_out.at[m], corr_in.at[m, distance - 1],
            (corr_sem.at[0, m, distance - 1], corr_sem.at[1, m, distance - 1]),
            {"tensor": peer(distance)},
        )

    def hop_copy(way, m):
        target = station + 1 if way == 0 else station - 1
        target = lax.rem(target + sections, sections)
        return remote(
            (next_h, next_g)[way].at[m], (hfull, gfull)[way].at[m, rank],
            (z_sem.at[way, 0, m], z_sem.at[way, 1, m]),
            {"section": target},
        )

    def spread(way, m):
        for distance in range(1, ranks):
            gather_copy(way, m, distance).start()

    gain_all[rank] = gains[...]
    for distance in range(1, ranks):
        gain_copy(distance).start()

    @pl.when(first)
    def _():
        for m in range(micro):
            hfull[m, rank] = hidden[m]
            spread(0, m)

    @pl.when(last)
    def _():
        for m in range(micro):
            gfull[m, rank] = grad_out[m]
            spread(1, m)

    for distance in range(1, ranks):
        gain_copy(distance).wait()

    def gather(way, m, at_source):
        @pl.when(jnp.logical_not(at_source))
        def _():
            hop_copy(way, m).wait_recv()
            spread(way, m)

        for distance in range(1, ranks):
            gather_copy(way, m, distance).wait()

    def gain_of(owner):
        return gain_all[owner][:1].astype(jnp.float32)

    def stack(block):
        return jnp.concatenate(
            [block[:, a * HEAD_DIM:(a + 1) * HEAD_DIM] for a in range(group)], 0
        )

    def head_parts(m, g):
        query = stack(queries[m, :, g * group * HEAD_DIM:(g + 1) * group * HEAD_DIM])
        key = keyval[m, :, 2 * g * HEAD_DIM:(2 * g + 1) * HEAD_DIM]
        value = keyval[m, :, (2 * g + 1) * HEAD_DIM:(2 * g + 2) * HEAD_DIM]
        return query, key, value

    def forward(m, carry):
        gather(0, m, first)
        line = pl.ds(pl.multiple_of(m * rows, rows), rows)
        total = jnp.zeros((rows, 1), jnp.float32)
        for owner in range(ranks):
            wide = hfull[m, owner].astype(jnp.float32)
            total = total + jnp.sum(wide * wide, -1, keepdims=True)
        scale = lax.rsqrt(total / model + EPS)
        scales[m] = jnp.broadcast_to(scale, (rows, HEAD_DIM))
        for owner in range(ranks):
            wide = hfull[m, owner].astype(jnp.float32)
            normed[line, owner * width:(owner + 1) * width] = (
                wide * scale * gain_of(owner)
            ).astype(jnp.bfloat16)

        @pl.when(m == 0)
        def _():
            loads[0].wait()
            loads[1].wait()

        def project_q(start, size):
            columns = pl.ds(start, size)
            queries[m, :, columns] = plain(normed[line, :], wq[:, columns]).astype(jnp.bfloat16)

        def project_kv(start, size):
            columns = pl.ds(start, size)
            keyval[m, :, columns] = plain(normed[line, :], wkv[:, columns]).astype(jnp.bfloat16)

        tiles(q_width, project_q)
        tiles(wkv.shape[1], project_kv)
        allowed = jnp.concatenate([mask[m]] * group, 0) > 0.5
        for g in range(pairs):
            query, key, value = head_parts(m, g)
            scores = outer_side(query, key) * HEAD_DIM ** (-0.5)
            scores = jnp.where(allowed, scores, NEG)
            raised = jnp.exp(scores - jnp.max(scores, -1, keepdims=True))
            attn = raised / jnp.sum(raised, -1, keepdims=True)
            weights[m, g] = attn
            mix = plain(attn.astype(jnp.bfloat16), value).astype(jnp.bfloat16)
            for a in range(group):
                at = (g * group + a) * HEAD_DIM
                mixed[line, at:at + HEAD_DIM] = mix[a * rows:(a + 1) * rows]

        @pl.when(m == 0)
        def _():
            loads[2].wait()

        @pl.when(jnp.logical_not(last))
        def _():
            for distance in range(1, ranks):
                base = peer(distance) * width

                def project_far(start, size):
                    far = pl.ds(pl.multiple_of(base + start, size), size)
                    send_f[m, distance - 1, :, pl.ds(start, size)] = plain(
                        mixed[line, :], wo[:, far]
                    ).astype(jnp.bfloat16)

                tiles(width, project_far)
                sum_copy(0, m, distance).start()

            def project_own(start, size):
                near = pl.ds(pl.multiple_of(rank * width + start, size), size)
                own[:, pl.ds(start, size)] = plain(mixed[line, :], wo[:, near])

            tiles(width, project_own)
            result = own[...]
            for distance in range(1, ranks):
                sum_copy(0, m, distance).wait()
                result = result + recv_f[m, distance - 1].astype(jnp.float32)
            next_h[m] = (hfull[m, rank].astype(jnp.float32) + result).astype(jnp.bfloat16)
            hop_copy(0, m).start()

        return carry

    lax.fori_loop(0, micro, forward, 0)
    gain_grad[...] = jnp.zeros(gain_grad.shape, jnp.float32)

    def backward(m, carry):
        gather(1, m, last)
        line = pl.ds(pl.multiple_of(m * rows, rows), rows)
        for owner in range(ranks):
            grad_rows[line, owner * width:(owner + 1) * width] = gfull[m, owner]

        def back_out(start, size):
            part = pl.ds(start, size)
            mix_grad[:, part] = outer_side(grad_rows[line, :], wo[part, :]).astype(jnp.bfloat16)

        tiles(q_width, back_out)
        for g in range(pairs):
            query, key, value = head_parts(m, g)
            attn = weights[m, g]
            grads = stack(mix_grad[:, g * group * HEAD_DIM:(g + 1) * group * HEAD_DIM])
            value_grad = inner(attn.astype(jnp.bfloat16), grads).astype(jnp.bfloat16)
            weight_grad = outer_side(grads, value)
            score_grad = (
                attn
                * (weight_grad - jnp.sum(weight_grad * attn, -1, keepdims=True))
                * HEAD_DIM ** (-0.5)
            ).astype(jnp.bfloat16)
            query_grad = plain(score_grad, key).astype(jnp.bfloat16)
            key_grad = inner(score_grad, query).astype(jnp.bfloat16)
            for a in range(group):
                at = (g * group + a) * HEAD_DIM
                pair_rows[line, at:at + HEAD_DIM] = query_grad[a * rows:(a + 1) * rows]
            at = q_width + 2 * g * HEAD_DIM
            pair_rows[line, at:at + HEAD_DIM] = key_grad
            pair_rows[line, at + HEAD_DIM:at + 2 * HEAD_DIM] = value_grad

        def back_in(base, start, size):
            part = pl.ds(pl.multiple_of(base + start, size), size)
            return outer_side(pair_rows[line, :q_width], wq[part, :]) + outer_side(
                pair_rows[line, q_width:], wkv[part, :]
            )

        corr_out[m] = jnp.zeros((rows, HEAD_DIM), jnp.float32)

        def correct(partial, owner, start, size):
            columns = pl.ds(start, size)
            gain = gain_all[owner, :, columns][:1].astype(jnp.float32)
            wide = hfull[m, owner, :, columns].astype(jnp.float32)
            corr_out[m] += jnp.broadcast_to(
                jnp.sum(partial * gain * wide, -1, keepdims=True), (rows, HEAD_DIM)
            )

        for distance in range(1, ranks):
            owner = peer(distance)

            def far(start, size):
                partial = back_in(owner * width, start, size)
                correct(partial, owner, start, size)
                send_b[m, distance - 1, :, pl.ds(start, size)] = partial.astype(jnp.bfloat16)

            tiles(width, far)
            sum_copy(1, m, distance).start()

        def near(start, size):
            partial = back_in(rank * width, start, size)
            correct(partial, rank, start, size)
            own[:, pl.ds(start, size)] = partial

        tiles(width, near)
        for distance in range(1, ranks):
            corr_copy(m, distance).start()
        normed_grad = own[...]
        for distance in range(1, ranks):
            sum_copy(1, m, distance).wait()
            normed_grad = normed_grad + recv_b[m, distance - 1].astype(jnp.float32)
        own[...] = normed_grad
        scale = scales[m][:, :1]
        wide = hfull[m, rank].astype(jnp.float32)
        gain_grad[...] += jnp.sum(own[...] * wide * scale, 0, keepdims=True)
        for distance in range(1, ranks):
            corr_copy(m, distance).wait()

        @pl.when(station > 0)
        def _():
            correction = corr_out[m]
            for distance in range(1, ranks):
                correction = correction + corr_in[m, distance - 1]
            factor = scale * scale * scale / model * correction[:, :1]
            next_g[m] = (
                gfull[m, rank].astype(jnp.float32)
                + scale * gain_of(rank) * own[...]
                - hfull[m, rank].astype(jnp.float32) * factor
            ).astype(jnp.bfloat16)
            hop_copy(1, m).start()

        return carry

    lax.fori_loop(0, micro, backward, 0)

    @pl.when(jnp.logical_not(last))
    def _():
        for m in range(micro):
            hop_copy(0, m).wait_send()

    @pl.when(station > 0)
    def _():
        for m in range(micro):
            hop_copy(1, m).wait_send()


def layers(hidden_in, mask, gains, query_weight, pair_weight, out_weight, grad_out):
    ranks, sections = lax.axis_size("tensor"), lax.axis_size("section")
    micro, rows, width = hidden_in.shape
    model = ranks * width
    q_width, kv_width = query_weight.shape[1], pair_weight.shape[1]
    pairs = kv_width // (2 * HEAD_DIM)
    group = q_width // (HEAD_DIM * pairs)
    half, wide = jnp.bfloat16, jnp.float32
    vmem = pl.BlockSpec(memory_space=pltpu.VMEM)
    anywhere = pl.BlockSpec(memory_space=pl.ANY)
    others = ranks - 1
    return pl.pallas_call(
        functools.partial(kernel, ranks, sections, micro),
        out_shape=(
            jax.ShapeDtypeStruct((micro * rows, model), half),
            jax.ShapeDtypeStruct((micro * rows, q_width), half),
            jax.ShapeDtypeStruct((micro * rows, q_width + kv_width), half),
            jax.ShapeDtypeStruct((micro * rows, model), half),
            jax.ShapeDtypeStruct((1, width), wide),
        ),
        in_specs=[vmem, vmem, vmem, anywhere, anywhere, anywhere, vmem],
        out_specs=(vmem,) * 5,
        scratch_shapes=[
            pltpu.VMEM((model, q_width), half),
            pltpu.VMEM((model, kv_width), half),
            pltpu.VMEM((q_width, model), half),
            pltpu.VMEM((micro, ranks, rows, width), half),
            pltpu.VMEM((micro, ranks, rows, width), half),
            pltpu.VMEM((ranks, 16, width), half),
            pltpu.VMEM((micro, rows, HEAD_DIM), wide),
            pltpu.VMEM((micro, rows, q_width), half),
            pltpu.VMEM((micro, rows, kv_width), half),
            pltpu.VMEM((micro, pairs, group * rows, rows), wide),
            pltpu.VMEM((rows, q_width), half),
            pltpu.VMEM((rows, width), wide),
            pltpu.VMEM((micro, others, rows, width), half),
            pltpu.VMEM((micro, others, rows, width), half),
            pltpu.VMEM((micro, others, rows, width), half),
            pltpu.VMEM((micro, others, rows, width), half),
            pltpu.VMEM((micro, rows, width), half),
            pltpu.VMEM((micro, rows, width), half),
            pltpu.VMEM((micro, rows, HEAD_DIM), wide),
            pltpu.VMEM((micro, others, rows, HEAD_DIM), wide),
            pltpu.SemaphoreType.DMA((3,)),
            pltpu.SemaphoreType.DMA((2, others)),
            pltpu.SemaphoreType.DMA((2, 2, micro, others)),
            pltpu.SemaphoreType.DMA((2, 2, micro, others)),
            pltpu.SemaphoreType.DMA((2, 2, micro)),
            pltpu.SemaphoreType.DMA((2, micro, others)),
        ],
        compiler_params=pltpu.CompilerParams(
            collective_id=0, has_side_effects=True, vmem_limit_bytes=60 << 20
        ),
    )(hidden_in, mask, gains, query_weight, pair_weight, out_weight, grad_out)


def shards(hidden_in, lengths, gains, w_query, w_keyval, w_out, grad_out):
    row_count = hidden_in.shape[1]
    query_weight = w_query[0]
    model_width = query_weight.shape[0]
    pair_count = w_keyval.shape[2]
    pair_weight = w_keyval[0].reshape(model_width, -1)
    position = jnp.arange(row_count)
    causal = position[None, :] <= position[:, None]
    mask = (causal[None] & (position[None, None, :] < lengths[:, None, None])).astype(jnp.float32)
    gain_rows = jnp.broadcast_to(gains, (16, gains.shape[1]))
    normed_rows, mixed_rows, pair_rows, outgrad_rows, gain_grad = layers(
        hidden_in, mask, gain_rows, query_weight, pair_weight, w_out[0], grad_out
    )
    mixed_rows = every_row(mixed_rows)
    output_total = inner(mixed_rows, own_columns(outgrad_rows))
    normed_rows = own_columns(normed_rows)
    pair_rows = every_row(pair_rows)
    query_width = query_weight.shape[1]
    query_total = inner(normed_rows, pair_rows[:, :query_width])
    pair_total = inner(normed_rows, pair_rows[:, query_width:])
    gain_total = lax.psum_scatter(gain_grad[0], "dp", scatter_dimension=0, tiled=True)
    grad_query = query_total[None]
    grad_keyval = pair_total.reshape(1, pair_total.shape[0], pair_count, 2 * HEAD_DIM)
    grad_outproj = output_total[None]
    grad_gain = gain_total[None]
    return (grad_query, grad_keyval, grad_outproj, grad_gain)


def solution(mesh):
    in_specs = (
        P("dp", None, "tensor"),
        P("dp"),
        P("section", "tensor"),
        P("section", None, "tensor"),
        P("section", None, "tensor", None),
        P("section", "tensor", None),
        P("dp", None, "tensor"),
    )
    out_specs = (
        P("section", "dp", "tensor"),
        P("section", "dp", "tensor", None),
        P("section", "tensor", "dp"),
        P("section", ("tensor", "dp")),
    )
    return jax.shard_map(shards, mesh=mesh, in_specs=in_specs, out_specs=out_specs, check_vma=False)
```

```python
import functools

import jax
import jax.numpy as jnp
from jax import lax
from jax.experimental import pallas as pl
from jax.experimental.pallas import tpu as pltpu
from jax.sharding import PartitionSpec as P

HEAD_DIM = 128


EPS = 1e-05
NEG = -1e30


def inner(former, latter):
    return lax.dot_general(
        former, latter, (((0,), (0,)), ((), ())), preferred_element_type=jnp.float32
    )


def outer_side(former, latter):
    return lax.dot_general(
        former, latter, (((1,), (1,)), ((), ())), preferred_element_type=jnp.float32
    )


def plain(former, latter):
    return jnp.dot(former, latter, preferred_element_type=jnp.float32)


def row_dot(former, latter):
    return jnp.sum(former.astype(jnp.float32) * latter.astype(jnp.float32), -1, keepdims=True)


def tile_of(width):
    return 512 if width % 512 == 0 else 256


def tiles(width, body):
    size = tile_of(width)

    def step(index, carry):
        body(pl.multiple_of(index * size, size), size)
        return carry

    lax.fori_loop(0, width // size, step, 0)


def kernel(
    ranks, sections, replicas, micro,
    hidden, mask, gains, wq_hbm, wkv_hbm, wo_hbm, grad_out,
    normed_all, mixed_all, pair_all, grad_all, gain_sum,
    normed, grad_rows, gain_grad,
    wq, wkv, wo, hfull, gfull, gain_all, scales, queries, keyval, weights, mix_grad,
    send_f, recv_f, send_b, recv_b, next_h, next_g, corr_out, corr_in,
    load_sem, gain_sem, ag_sem, rs_sem, z_sem, corr_sem, cut_sem, line_sem, core_sem, sum_sem,
):
    rank = lax.axis_index("tensor")
    station = lax.axis_index("section")
    rows = hidden.shape[1]
    width = hidden.shape[2]
    model = ranks * width
    q_width = wq.shape[1]
    pairs = wkv.shape[1] // (2 * HEAD_DIM)
    group = q_width // (HEAD_DIM * pairs)
    chunk = tile_of(width)
    chunks = width // chunk
    mixed, pair_rows = mixed_all.at[0], pair_all.at[0]
    replica = lax.axis_index("dp")
    lines = replicas // 2
    slots = [(d, c) for c in (0, 1) for d in range(lines)]
    cut = model // replicas
    first, last = station == 0, station == sections - 1

    def peer(distance):
        return lax.rem(rank + distance, ranks)

    def twin(slot):
        line = lax.rem(lax.div(replica, 2) + slot[0], lines)
        core = lax.rem(replica + slot[1], 2)
        return line * 2 + core

    def remote(source, target, sems, device):
        return pltpu.make_async_remote_copy(
            src_ref=source, dst_ref=target, send_sem=sems[0], recv_sem=sems[1],
            device_id=device, device_id_type=pl.DeviceIdType.MESH,
        )

    barrier = pltpu.get_barrier_semaphore()
    for distance in range(1, ranks):
        pl.semaphore_signal(
            barrier, inc=1, device_id={"tensor": peer(distance)},
            device_id_type=pl.DeviceIdType.MESH,
        )

    for slot in slots[1:]:
        pl.semaphore_signal(
            barrier, inc=1, device_id={"dp": twin(slot)},
            device_id_type=pl.DeviceIdType.MESH,
        )

    @pl.when(station > 0)
    def _():
        pl.semaphore_signal(
            barrier, inc=1, device_id={"section": station - 1},
            device_id_type=pl.DeviceIdType.MESH,
        )

    @pl.when(station < sections - 1)
    def _():
        pl.semaphore_signal(
            barrier, inc=1, device_id={"section": station + 1},
            device_id_type=pl.DeviceIdType.MESH,
        )

    loads = [
        pltpu.make_async_copy(source, target, load_sem.at[index])
        for index, (source, target) in enumerate(((wq_hbm, wq), (wkv_hbm, wkv), (wo_hbm, wo)))
    ]

    def source_copy(way, m):
        return pltpu.make_async_copy(
            (hidden, grad_out)[way].at[m], (hfull, gfull)[way].at[m, rank],
            load_sem.at[3 + way * micro + m],
        )

    @pl.when(first)
    def _():
        for m in range(micro):
            source_copy(0, m).start()

    @pl.when(last)
    def _():
        for m in range(micro):
            source_copy(1, m).start()

    for load in loads:
        load.start()

    ends = jnp.where(first, 0, 1) + jnp.where(last, 0, 1)
    pl.semaphore_wait(barrier, ranks - 1 + replicas - 1 + ends)

    def gain_copy(distance):
        return remote(
            gain_all.at[rank], gain_all.at[rank],
            (gain_sem.at[0, distance - 1], gain_sem.at[1, distance - 1]),
            {"tensor": peer(distance)},
        )

    def columns_of(index):
        return pl.ds(pl.multiple_of(index * chunk, chunk), chunk)

    def gather_copy(way, m, index, distance):
        block = (hfull, gfull)[way].at[m, rank, :, columns_of(index)]
        return remote(
            block, block,
            (ag_sem.at[way, 0, m, index, distance - 1], ag_sem.at[way, 1, m, index, distance - 1]),
            {"tensor": peer(distance)},
        )

    def sum_copy(way, m, index, distance):
        columns = columns_of(index)
        return remote(
            (send_f, send_b)[way].at[m, distance - 1, :, columns],
            (recv_f, recv_b)[way].at[m, distance - 1, :, columns],
            (rs_sem.at[way, 0, m, index, distance - 1], rs_sem.at[way, 1, m, index, distance - 1]),
            {"tensor": peer(distance)},
        )

    def corr_copy(m, distance):
        return remote(
            corr_out.at[m], corr_in.at[m, distance - 1],
            (corr_sem.at[0, m, distance - 1], corr_sem.at[1, m, distance - 1]),
            {"tensor": peer(distance)},
        )

    def hop_copy(way, m, index):
        target = station + 1 if way == 0 else station - 1
        target = lax.rem(target + sections, sections)
        columns = columns_of(index)
        return remote(
            (next_h, next_g)[way].at[m, :, columns],
            (hfull, gfull)[way].at[m, rank, :, columns],
            (z_sem.at[way, 0, m, index], z_sem.at[way, 1, m, index]),
            {"section": target},
        )

    def spread(way, m, index):
        for distance in range(1, ranks):
            gather_copy(way, m, index, distance).start()

    def line_of(m):
        return pl.ds(pl.multiple_of(m * rows, rows), rows)

    def cut_copy(kind, m, place):
        target = twin(slots[place])
        source = (normed, grad_rows)[kind]
        return remote(
            source.at[line_of(m), pl.ds(pl.multiple_of(target * cut, cut), cut)],
            (normed_all, grad_all)[kind].at[place, line_of(m)],
            (cut_sem.at[kind, 0, m, place - 1], cut_sem.at[kind, 1, m, place - 1]),
            {"dp": target},
        )

    def start_cut(kind, m):
        own_cut = pl.ds(pl.multiple_of(replica * cut, cut), cut)
        (normed_all, grad_all)[kind][0, line_of(m)] = (normed, grad_rows)[kind][line_of(m), own_cut]
        for place in range(1, replicas):
            cut_copy(kind, m, place).start()

    def line_copy(kind, m, place):
        whole = (mixed_all, pair_all)[kind]
        return remote(
            whole.at[0, line_of(m)], whole.at[place, line_of(m)],
            (line_sem.at[kind, 0, m, place - 1], line_sem.at[kind, 1, m, place - 1]),
            {"dp": twin((place, 0))},
        )

    def core_copy(kind, m, place):
        whole = (mixed_all, pair_all)[kind]
        return remote(
            whole.at[place, line_of(m)], whole.at[lines + place, line_of(m)],
            (core_sem.at[kind, 0, m, place], core_sem.at[kind, 1, m, place]),
            {"dp": twin((0, 1))},
        )

    def start_rows(kind, m):
        for place in range(1, lines):
            line_copy(kind, m, place).start()
        core_copy(kind, m, 0).start()

    def pass_rows(kind, m):
        for place in range(1, lines):
            line_copy(kind, m, place).wait_recv()
            core_copy(kind, m, place).start()

    def total_copy(place):
        return remote(
            gain_grad.at[0], gain_grad.at[place],
            (sum_sem.at[0, place - 1], sum_sem.at[1, place - 1]),
            {"dp": twin(slots[place])},
        )

    gain_all[rank] = gains[...]
    for distance in range(1, ranks):
        gain_copy(distance).start()

    @pl.when(first)
    def _():
        for m in range(micro):
            source_copy(0, m).wait()
            for index in range(chunks):
                spread(0, m, index)

    @pl.when(last)
    def _():
        for m in range(micro):
            source_copy(1, m).wait()
            for index in range(chunks):
                spread(1, m, index)

    for distance in range(1, ranks):
        gain_copy(distance).wait()

    def gather(way, m, at_source):
        @pl.when(jnp.logical_not(at_source))
        def _():
            for index in range(chunks):
                hop_copy(way, m, index).wait_recv()
                spread(way, m, index)

        for index in range(chunks):
            for distance in range(1, ranks):
                gather_copy(way, m, index, distance).wait()

    def gain_of(owner):
        return gain_all[owner][:1].astype(jnp.float32)

    def stack(block):
        return jnp.concatenate(
            [block[:, a * HEAD_DIM:(a + 1) * HEAD_DIM] for a in range(group)], 0
        )

    def head_parts(m, g):
        query = stack(queries[m, :, g * group * HEAD_DIM:(g + 1) * group * HEAD_DIM])
        key = keyval[m, :, 2 * g * HEAD_DIM:(2 * g + 1) * HEAD_DIM]
        value = keyval[m, :, (2 * g + 1) * HEAD_DIM:(2 * g + 2) * HEAD_DIM]
        return query, key, value

    def forward(m, carry):
        gather(0, m, first)
        line = line_of(m)
        total = jnp.zeros((rows, 1), jnp.float32)
        for owner in range(ranks):
            wide = hfull[m, owner].astype(jnp.float32)
            total = total + jnp.sum(wide * wide, -1, keepdims=True)
        scale = lax.rsqrt(total / model + EPS)
        scales[m] = jnp.broadcast_to(scale, (rows, HEAD_DIM))
        for owner in range(ranks):
            wide = hfull[m, owner].astype(jnp.float32)
            normed[line, owner * width:(owner + 1) * width] = (
                wide * scale * gain_of(owner)
            ).astype(jnp.bfloat16)

        start_cut(0, m)

        @pl.when(m == 0)
        def _():
            loads[0].wait()
            loads[1].wait()

        def project_q(start, size):
            columns = pl.ds(start, size)
            queries[m, :, columns] = plain(normed[line, :], wq[:, columns]).astype(jnp.bfloat16)

        def project_kv(start, size):
            columns = pl.ds(start, size)
            keyval[m, :, columns] = plain(normed[line, :], wkv[:, columns]).astype(jnp.bfloat16)

        tiles(q_width, project_q)
        tiles(wkv.shape[1], project_kv)
        allowed = jnp.concatenate([mask[m]] * group, 0) > 0.5
        for g in range(pairs):
            query, key, value = head_parts(m, g)
            scores = outer_side(query, key) * HEAD_DIM ** (-0.5)
            scores = jnp.where(allowed, scores, NEG)
            raised = jnp.exp(scores - jnp.max(scores, -1, keepdims=True))
            attn = raised / jnp.sum(raised, -1, keepdims=True)
            weights[m, g] = attn
            mix = plain(attn.astype(jnp.bfloat16), value).astype(jnp.bfloat16)
            for a in range(group):
                at = (g * group + a) * HEAD_DIM
                mixed[line, at:at + HEAD_DIM] = mix[a * rows:(a + 1) * rows]

        start_rows(0, m)

        @pl.when(m == 0)
        def _():
            loads[2].wait()

        @pl.when(jnp.logical_not(last))
        def _():
            for distance in range(1, ranks):
                base = peer(distance) * width

                def project_far(start, size):
                    far = pl.ds(pl.multiple_of(base + start, size), size)
                    send_f[m, distance - 1, :, pl.ds(start, size)] = plain(
                        mixed[line, :], wo[:, far]
                    ).astype(jnp.bfloat16)
                    sum_copy(0, m, lax.div(start, size), distance).start()

                tiles(width, project_far)

            def project_own(start, size):
                near = pl.ds(pl.multiple_of(rank * width + start, size), size)
                index, columns = lax.div(start, size), pl.ds(start, size)
                result = plain(mixed[line, :], wo[:, near])
                for distance in range(1, ranks):
                    sum_copy(0, m, index, distance).wait()
                    result = result + recv_f[m, distance - 1, :, columns].astype(jnp.float32)
                next_h[m, :, columns] = (
                    hfull[m, rank, :, columns].astype(jnp.float32) + result
                ).astype(jnp.bfloat16)
                hop_copy(0, m, index).start()

            tiles(width, project_own)

        return carry

    lax.fori_loop(0, micro, forward, 0)
    gain_grad[0] = jnp.zeros(gain_grad.shape[1:], jnp.float32)

    def backward(m, carry):
        gather(1, m, last)
        line = line_of(m)
        for owner in range(ranks):
            grad_rows[line, owner * width:(owner + 1) * width] = gfull[m, owner]
        start_cut(1, m)

        def back_out(start, size):
            part = pl.ds(start, size)
            mix_grad[:, part] = outer_side(grad_rows[line, :], wo[part, :]).astype(jnp.bfloat16)

        tiles(q_width, back_out)
        correction = jnp.zeros((rows, 1), jnp.float32)
        for g in range(pairs):
            query, key, value = head_parts(m, g)
            attn = weights[m, g]
            grads = stack(mix_grad[:, g * group * HEAD_DIM:(g + 1) * group * HEAD_DIM])
            value_grad = inner(attn.astype(jnp.bfloat16), grads).astype(jnp.bfloat16)
            weight_grad = outer_side(grads, value)
            score_grad = (
                attn
                * (weight_grad - jnp.sum(weight_grad * attn, -1, keepdims=True))
                * HEAD_DIM ** (-0.5)
            ).astype(jnp.bfloat16)
            query_grad = plain(score_grad, key).astype(jnp.bfloat16)
            key_grad = inner(score_grad, query).astype(jnp.bfloat16)
            query_part = row_dot(query_grad, query)
            correction = correction + row_dot(key_grad, key) + row_dot(value_grad, value)
            for a in range(group):
                correction = correction + query_part[a * rows:(a + 1) * rows]
                at = (g * group + a) * HEAD_DIM
                pair_rows[line, at:at + HEAD_DIM] = query_grad[a * rows:(a + 1) * rows]
            at = q_width + 2 * g * HEAD_DIM
            pair_rows[line, at:at + HEAD_DIM] = key_grad
            pair_rows[line, at + HEAD_DIM:at + 2 * HEAD_DIM] = value_grad

        def back_in(base, start, size):
            part = pl.ds(pl.multiple_of(base + start, size), size)
            return outer_side(pair_rows[line, :q_width], wq[part, :]) + outer_side(
                pair_rows[line, q_width:], wkv[part, :]
            )

        scale = scales[m][:, :1]
        corr_out[m] = jnp.broadcast_to(correction / scale, (rows, HEAD_DIM))
        for distance in range(1, ranks):
            corr_copy(m, distance).start()
        start_rows(1, m)

        for distance in range(1, ranks):
            owner = peer(distance)

            def far(start, size):
                partial = back_in(owner * width, start, size)
                send_b[m, distance - 1, :, pl.ds(start, size)] = partial.astype(jnp.bfloat16)
                sum_copy(1, m, lax.div(start, size), distance).start()

            tiles(width, far)

        total = corr_out[m]
        for distance in range(1, ranks):
            corr_copy(m, distance).wait()
            total = total + corr_in[m, distance - 1]
        factor = scale * scale * scale / model * total[:, :1]

        def near(start, size):
            index, columns = lax.div(start, size), pl.ds(start, size)
            partial = back_in(rank * width, start, size)
            for distance in range(1, ranks):
                sum_copy(1, m, index, distance).wait()
                partial = partial + recv_b[m, distance - 1, :, columns].astype(jnp.float32)
            wide = hfull[m, rank, :, columns].astype(jnp.float32)
            gain = gain_all[rank, :, columns][:1].astype(jnp.float32)

            @pl.when(station > 0)
            def _():
                next_g[m, :, columns] = (
                    gfull[m, rank, :, columns].astype(jnp.float32)
                    + scale * gain * partial
                    - wide * factor
                ).astype(jnp.bfloat16)
                hop_copy(1, m, index).start()

            gain_grad[0, :, columns] += jnp.broadcast_to(
                jnp.sum(partial * wide * scale, 0, keepdims=True), (8, size)
            )

        tiles(width, near)
        pass_rows(0, m)
        pass_rows(1, m)
        return carry

    lax.fori_loop(0, micro, backward, 0)
    for place in range(1, replicas):
        total_copy(place).start()
    for m in range(micro):
        for kind in range(2):
            for place in range(1, replicas):
                cut_copy(kind, m, place).wait()
            for place in range(1, lines):
                line_copy(kind, m, place).wait_send()
            for place in range(lines):
                core_copy(kind, m, place).wait()
    total = gain_grad[0]
    for place in range(1, replicas):
        total_copy(place).wait()
        total = total + gain_grad[place]
    gain_sum[...] = total

    @pl.when(jnp.logical_not(last))
    def _():
        for m in range(micro):
            for index in range(chunks):
                hop_copy(0, m, index).wait_send()

    @pl.when(station > 0)
    def _():
        for m in range(micro):
            for index in range(chunks):
                hop_copy(1, m, index).wait_send()


def layers(hidden_in, mask, gains, query_weight, pair_weight, out_weight, grad_out):
    ranks, sections = lax.axis_size("tensor"), lax.axis_size("section")
    replicas = lax.axis_size("dp")
    micro, rows, width = hidden_in.shape
    model = ranks * width
    q_width, kv_width = query_weight.shape[1], pair_weight.shape[1]
    pairs = kv_width // (2 * HEAD_DIM)
    group = q_width // (HEAD_DIM * pairs)
    half, wide = jnp.bfloat16, jnp.float32
    vmem = pl.BlockSpec(memory_space=pltpu.VMEM)
    anywhere = pl.BlockSpec(memory_space=pl.ANY)
    others, lines, chunks = ranks - 1, replicas // 2, width // tile_of(width)
    return pl.pallas_call(
        functools.partial(kernel, ranks, sections, replicas, micro),
        out_shape=(
            jax.ShapeDtypeStruct((replicas, micro * rows, model // replicas), half),
            jax.ShapeDtypeStruct((replicas, micro * rows, q_width), half),
            jax.ShapeDtypeStruct((replicas, micro * rows, q_width + kv_width), half),
            jax.ShapeDtypeStruct((replicas, micro * rows, model // replicas), half),
            jax.ShapeDtypeStruct((8, width), wide),
        ),
        in_specs=[anywhere, vmem, vmem, anywhere, anywhere, anywhere, anywhere],
        out_specs=(vmem,) * 5,
        scratch_shapes=[
            pltpu.VMEM((micro * rows, model), half),
            pltpu.VMEM((micro * rows, model), half),
            pltpu.VMEM((replicas, 8, width), wide),
            pltpu.VMEM((model, q_width), half),
            pltpu.VMEM((model, kv_width), half),
            pltpu.VMEM((q_width, model), half),
            pltpu.VMEM((micro, ranks, rows, width), half),
            pltpu.VMEM((micro, ranks, rows, width), half),
            pltpu.VMEM((ranks, 16, width), half),
            pltpu.VMEM((micro, rows, HEAD_DIM), wide),
            pltpu.VMEM((micro, rows, q_width), half),
            pltpu.VMEM((micro, rows, kv_width), half),
            pltpu.VMEM((micro, pairs, group * rows, rows), wide),
            pltpu.VMEM((rows, q_width), half),
            pltpu.VMEM((micro, others, rows, width), half),
            pltpu.VMEM((micro, others, rows, width), half),
            pltpu.VMEM((micro, others, rows, width), half),
            pltpu.VMEM((micro, others, rows, width), half),
            pltpu.VMEM((micro, rows, width), half),
            pltpu.VMEM((micro, rows, width), half),
            pltpu.VMEM((micro, rows, HEAD_DIM), wide),
            pltpu.VMEM((micro, others, rows, HEAD_DIM), wide),
            pltpu.SemaphoreType.DMA((3 + 2 * micro,)),
            pltpu.SemaphoreType.DMA((2, others)),
            pltpu.SemaphoreType.DMA((2, 2, micro, chunks, others)),
            pltpu.SemaphoreType.DMA((2, 2, micro, chunks, others)),
            pltpu.SemaphoreType.DMA((2, 2, micro, chunks)),
            pltpu.SemaphoreType.DMA((2, micro, others)),
            pltpu.SemaphoreType.DMA((2, 2, micro, replicas - 1)),
            pltpu.SemaphoreType.DMA((2, 2, micro, max(lines - 1, 1))),
            pltpu.SemaphoreType.DMA((2, 2, micro, lines)),
            pltpu.SemaphoreType.DMA((2, replicas - 1)),
        ],
        compiler_params=pltpu.CompilerParams(
            collective_id=0, has_side_effects=True, vmem_limit_bytes=60 << 20
        ),
    )(hidden_in, mask, gains, query_weight, pair_weight, out_weight, grad_out)


def shards(hidden_in, lengths, gains, w_query, w_keyval, w_out, grad_out):
    row_count = hidden_in.shape[1]
    query_weight = w_query[0]
    model_width = query_weight.shape[0]
    pair_count = w_keyval.shape[2]
    pair_weight = w_keyval[0].reshape(model_width, -1)
    position = jnp.arange(row_count)
    causal = position[None, :] <= position[:, None]
    mask = (causal[None] & (position[None, None, :] < lengths[:, None, None])).astype(jnp.float32)
    gain_rows = jnp.broadcast_to(gains, (16, gains.shape[1]))
    *gathered, gain_sum = layers(
        hidden_in, mask, gain_rows, query_weight, pair_weight, w_out[0], grad_out
    )
    normed_rows, mixed_rows, pair_rows, outgrad_rows = [
        block.reshape(-1, block.shape[2]) for block in gathered
    ]
    query_width = query_weight.shape[1]
    query_total = inner(normed_rows, pair_rows[:, :query_width])
    pair_total = inner(normed_rows, pair_rows[:, query_width:])
    output_total = inner(mixed_rows, outgrad_rows)
    gain_width = gain_sum.shape[1] // lax.axis_size("dp")
    gain_total = lax.dynamic_slice_in_dim(gain_sum[0], lax.axis_index("dp") * gain_width, gain_width)
    grad_query = query_total[None]
    grad_keyval = pair_total.reshape(1, pair_total.shape[0], pair_count, 2 * HEAD_DIM)
    grad_outproj = output_total[None]
    grad_gain = gain_total[None]
    return (grad_query, grad_keyval, grad_outproj, grad_gain)


def solution(mesh):
    in_specs = (
        P("dp", None, "tensor"),
        P("dp"),
        P("section", "tensor"),
        P("section", None, "tensor"),
        P("section", None, "tensor", None),
        P("section", "tensor", None),
        P("dp", None, "tensor"),
    )
    out_specs = (
        P("section", "dp", "tensor"),
        P("section", "dp", "tensor", None),
        P("section", "tensor", "dp"),
        P("section", ("tensor", "dp")),
    )
    return jax.shard_map(shards, mesh=mesh, in_specs=in_specs, out_specs=out_specs, check_vma=False)
```

```python
import functools

import jax
import jax.numpy as jnp
from jax import lax
from jax.experimental import pallas as pl
from jax.experimental.pallas import tpu as pltpu
from jax.sharding import PartitionSpec as P

HEAD_DIM = 128


EPS = 1e-05
NEG = -1e30


def inner(former, latter):
    return lax.dot_general(
        former, latter, (((0,), (0,)), ((), ())), preferred_element_type=jnp.float32
    )


def outer_side(former, latter):
    return lax.dot_general(
        former, latter, (((1,), (1,)), ((), ())), preferred_element_type=jnp.float32
    )


def plain(former, latter):
    return jnp.dot(former, latter, preferred_element_type=jnp.float32)


def row_dot(former, latter):
    return jnp.sum(former.astype(jnp.float32) * latter.astype(jnp.float32), -1, keepdims=True)


def tile_of(width):
    return 512 if width % 512 == 0 else 256


def tiles(width, body):
    size = tile_of(width)

    def step(index, carry):
        body(pl.multiple_of(index * size, size), size)
        return carry

    lax.fori_loop(0, width // size, step, 0)


def kernel(
    ranks, sections, replicas, micro,
    hidden, mask, gains, wq_hbm, wkv_hbm, wo_hbm, grad_out,
    normed_all, mixed_all, pair_all, grad_all, gain_sum,
    normed, gain_grad, acc,
    wq, wkv, wo, hfull, gfull, gain_all, scales, queries, keyval, weights, mix_grad,
    send_f, recv_f, send_b, recv_b, next_h, next_g, corr_out, corr_in,
    load_sem, gain_sem, ag_sem, rs_sem, z_sem, corr_sem, cut_sem, line_sem, core_sem, sum_sem,
):
    rank = lax.axis_index("tensor")
    station = lax.axis_index("section")
    rows = hidden.shape[1]
    width = hidden.shape[2]
    model = ranks * width
    q_width = wq.shape[1]
    pairs = wkv.shape[1] // (2 * HEAD_DIM)
    group = q_width // (HEAD_DIM * pairs)
    chunk = tile_of(width)
    chunks = width // chunk
    mixed, pair_rows = mixed_all.at[0], pair_all.at[0]
    replica = lax.axis_index("dp")
    lines = replicas // 2
    slots = [(d, c) for c in (0, 1) for d in range(lines)]
    cut = model // replicas
    first, last = station == 0, station == sections - 1

    def peer(distance):
        return lax.rem(rank + distance, ranks)

    def twin(slot):
        line = lax.rem(lax.div(replica, 2) + slot[0], lines)
        core = lax.rem(replica + slot[1], 2)
        return line * 2 + core

    def remote(source, target, sems, device):
        return pltpu.make_async_remote_copy(
            src_ref=source, dst_ref=target, send_sem=sems[0], recv_sem=sems[1],
            device_id=device, device_id_type=pl.DeviceIdType.MESH,
        )

    barrier = pltpu.get_barrier_semaphore()
    for distance in range(1, ranks):
        pl.semaphore_signal(
            barrier, inc=1, device_id={"tensor": peer(distance)},
            device_id_type=pl.DeviceIdType.MESH,
        )

    for slot in slots[1:]:
        pl.semaphore_signal(
            barrier, inc=1, device_id={"dp": twin(slot)},
            device_id_type=pl.DeviceIdType.MESH,
        )

    @pl.when(station > 0)
    def _():
        pl.semaphore_signal(
            barrier, inc=1, device_id={"section": station - 1},
            device_id_type=pl.DeviceIdType.MESH,
        )

    @pl.when(station < sections - 1)
    def _():
        pl.semaphore_signal(
            barrier, inc=1, device_id={"section": station + 1},
            device_id_type=pl.DeviceIdType.MESH,
        )

    loads = [
        pltpu.make_async_copy(source, target, load_sem.at[index])
        for index, (source, target) in enumerate(((wq_hbm, wq), (wkv_hbm, wkv), (wo_hbm, wo)))
    ]

    def source_copy(way, m):
        return pltpu.make_async_copy(
            (hidden, grad_out)[way].at[m], (hfull, gfull)[way].at[m, rank],
            load_sem.at[3 + way * micro + m],
        )

    @pl.when(first)
    def _():
        for m in range(micro):
            source_copy(0, m).start()

    @pl.when(last)
    def _():
        for m in range(micro):
            source_copy(1, m).start()

    for load in loads:
        load.start()

    ends = jnp.where(first, 0, 1) + jnp.where(last, 0, 1)
    pl.semaphore_wait(barrier, ranks - 1 + replicas - 1 + ends)

    def gain_copy(distance):
        return remote(
            gain_all.at[rank], gain_all.at[rank],
            (gain_sem.at[0, distance - 1], gain_sem.at[1, distance - 1]),
            {"tensor": peer(distance)},
        )

    def columns_of(index):
        return pl.ds(pl.multiple_of(index * chunk, chunk), chunk)

    def gather_copy(way, m, index, distance):
        block = (hfull, gfull)[way].at[m, rank, :, columns_of(index)]
        return remote(
            block, block,
            (ag_sem.at[way, 0, m, index, distance - 1], ag_sem.at[way, 1, m, index, distance - 1]),
            {"tensor": peer(distance)},
        )

    def sum_copy(way, m, index, distance):
        columns = columns_of(index)
        return remote(
            (send_f, send_b)[way].at[m, distance - 1, :, columns],
            (recv_f, recv_b)[way].at[m, distance - 1, :, columns],
            (rs_sem.at[way, 0, m, index, distance - 1], rs_sem.at[way, 1, m, index, distance - 1]),
            {"tensor": peer(distance)},
        )

    def corr_copy(m, distance):
        return remote(
            corr_out.at[m], corr_in.at[m, distance - 1],
            (corr_sem.at[0, m, distance - 1], corr_sem.at[1, m, distance - 1]),
            {"tensor": peer(distance)},
        )

    def hop_copy(way, m, index):
        target = station + 1 if way == 0 else station - 1
        target = lax.rem(target + sections, sections)
        columns = columns_of(index)
        return remote(
            (next_h, next_g)[way].at[m, :, columns],
            (hfull, gfull)[way].at[m, rank, :, columns],
            (z_sem.at[way, 0, m, index], z_sem.at[way, 1, m, index]),
            {"section": target},
        )

    def spread(way, m, index):
        for distance in range(1, ranks):
            gather_copy(way, m, index, distance).start()

    def line_of(m):
        return pl.ds(pl.multiple_of(m * rows, rows), rows)

    def cut_of(kind, m, target):
        if kind == 0:
            return normed.at[line_of(m), pl.ds(pl.multiple_of(target * cut, cut), cut)]
        start = lax.rem(target * cut, width)
        return gfull.at[m, lax.div(target * cut, width), :, pl.ds(pl.multiple_of(start, cut), cut)]

    def cut_copy(kind, m, place):
        target = twin(slots[place])
        return remote(
            cut_of(kind, m, target),
            (normed_all, grad_all)[kind].at[place, line_of(m)],
            (cut_sem.at[kind, 0, m, place - 1], cut_sem.at[kind, 1, m, place - 1]),
            {"dp": target},
        )

    def start_cut(kind, m):
        (normed_all, grad_all)[kind][0, line_of(m)] = cut_of(kind, m, replica)[...]
        for place in range(1, replicas):
            cut_copy(kind, m, place).start()

    def line_copy(kind, m, place):
        whole = (mixed_all, pair_all)[kind]
        return remote(
            whole.at[0, line_of(m)], whole.at[place, line_of(m)],
            (line_sem.at[kind, 0, m, place - 1], line_sem.at[kind, 1, m, place - 1]),
            {"dp": twin((place, 0))},
        )

    def core_copy(kind, m, place):
        whole = (mixed_all, pair_all)[kind]
        return remote(
            whole.at[place, line_of(m)], whole.at[lines + place, line_of(m)],
            (core_sem.at[kind, 0, m, place], core_sem.at[kind, 1, m, place]),
            {"dp": twin((0, 1))},
        )

    def start_rows(kind, m):
        for place in range(1, lines):
            line_copy(kind, m, place).start()
        core_copy(kind, m, 0).start()

    def pass_rows(kind, m):
        for place in range(1, lines):
            line_copy(kind, m, place).wait_recv()
            core_copy(kind, m, place).start()

    def total_copy(place):
        return remote(
            gain_grad.at[0], gain_grad.at[place],
            (sum_sem.at[0, place - 1], sum_sem.at[1, place - 1]),
            {"dp": twin(slots[place])},
        )

    gain_all[rank] = gains[...]
    for distance in range(1, ranks):
        gain_copy(distance).start()

    @pl.when(first)
    def _():
        for m in range(micro):
            source_copy(0, m).wait()
            for index in range(chunks):
                spread(0, m, index)

    @pl.when(last)
    def _():
        for m in range(micro):
            source_copy(1, m).wait()
            for index in range(chunks):
                spread(1, m, index)

    for distance in range(1, ranks):
        gain_copy(distance).wait()

    def gather(way, m, at_source, use):
        def near(index, carry):
            @pl.when(jnp.logical_not(at_source))
            def _():
                hop_copy(way, m, index).wait_recv()
                spread(way, m, index)

            use(rank, columns_of(index), features_of(rank, index))
            return carry

        acc[...] = jnp.zeros(acc.shape, jnp.float32)
        lax.fori_loop(0, chunks, near, 0)
        for distance in range(1, ranks):
            owner = lax.rem(rank - distance + ranks, ranks)

            def far(index, carry, distance=distance, owner=owner):
                gather_copy(way, m, index, distance).wait()
                use(owner, columns_of(index), features_of(owner, index))
                return carry

            lax.fori_loop(0, chunks, far, 0)

    def features_of(owner, index):
        return pl.ds(pl.multiple_of(owner * width + index * chunk, chunk), chunk)

    def gain_of(owner):
        return gain_all[owner][:1].astype(jnp.float32)

    def stack(block):
        return jnp.concatenate(
            [block[:, a * HEAD_DIM:(a + 1) * HEAD_DIM] for a in range(group)], 0
        )

    def head_parts(m, g):
        query = stack(queries[m, :, g * group * HEAD_DIM:(g + 1) * group * HEAD_DIM])
        key = keyval[m, :, 2 * g * HEAD_DIM:(2 * g + 1) * HEAD_DIM]
        value = keyval[m, :, (2 * g + 1) * HEAD_DIM:(2 * g + 2) * HEAD_DIM]
        return query, key, value

    def forward(m, carry):
        line = line_of(m)

        @pl.when(m == 0)
        def _():
            loads[0].wait()
            loads[1].wait()

        scales[m] = jnp.zeros((rows, HEAD_DIM), jnp.float32)

        def project(owner, columns, part):
            wide = hfull[m, owner, :, columns].astype(jnp.float32)
            scales[m] += jnp.broadcast_to(
                jnp.sum(wide * wide, -1, keepdims=True), (rows, HEAD_DIM)
            )
            gain = gain_all[owner, :, columns][:1].astype(jnp.float32)
            raised = (wide * gain).astype(jnp.bfloat16)
            acc[:, :q_width] += plain(raised, wq[part, :])
            acc[:, q_width:] += plain(raised, wkv[part, :])

        gather(0, m, first, project)
        scale = lax.rsqrt(scales[m][:, :1] / model + EPS)
        scales[m] = jnp.broadcast_to(scale, (rows, HEAD_DIM))
        queries[m] = (acc[:, :q_width] * scale).astype(jnp.bfloat16)
        keyval[m] = (acc[:, q_width:] * scale).astype(jnp.bfloat16)
        allowed = jnp.concatenate([mask[m]] * group, 0) > 0.5
        for g in range(pairs):
            query, key, value = head_parts(m, g)
            scores = outer_side(query, key) * HEAD_DIM ** (-0.5)
            scores = jnp.where(allowed, scores, NEG)
            raised = jnp.exp(scores - jnp.max(scores, -1, keepdims=True))
            attn = raised / jnp.sum(raised, -1, keepdims=True)
            weights[m, g] = attn
            mix = plain(attn.astype(jnp.bfloat16), value).astype(jnp.bfloat16)
            for a in range(group):
                at = (g * group + a) * HEAD_DIM
                mixed[line, at:at + HEAD_DIM] = mix[a * rows:(a + 1) * rows]

        start_rows(0, m)

        @pl.when(m == 0)
        def _():
            loads[2].wait()

        @pl.when(jnp.logical_not(last))
        def _():
            for distance in range(1, ranks):
                base = peer(distance) * width

                def project_far(start, size):
                    far = pl.ds(pl.multiple_of(base + start, size), size)
                    send_f[m, distance - 1, :, pl.ds(start, size)] = plain(
                        mixed[line, :], wo[:, far]
                    ).astype(jnp.bfloat16)
                    sum_copy(0, m, lax.div(start, size), distance).start()

                tiles(width, project_far)

            def project_own(start, size):
                near = pl.ds(pl.multiple_of(rank * width + start, size), size)
                index, columns = lax.div(start, size), pl.ds(start, size)
                result = plain(mixed[line, :], wo[:, near])
                for distance in range(1, ranks):
                    sum_copy(0, m, index, distance).wait()
                    result = result + recv_f[m, distance - 1, :, columns].astype(jnp.float32)
                next_h[m, :, columns] = (
                    hfull[m, rank, :, columns].astype(jnp.float32) + result
                ).astype(jnp.bfloat16)
                hop_copy(0, m, index).start()

            tiles(width, project_own)

        for owner in range(ranks):
            wide = hfull[m, owner].astype(jnp.float32)
            normed[line, owner * width:(owner + 1) * width] = (
                wide * scale * gain_of(owner)
            ).astype(jnp.bfloat16)
        start_cut(0, m)
        return carry

    lax.fori_loop(0, micro, forward, 0)
    gain_grad[0] = jnp.zeros(gain_grad.shape[1:], jnp.float32)

    def backward(m, carry):
        line = line_of(m)

        def back_out(owner, columns, part):
            acc[:, :q_width] += outer_side(gfull[m, owner, :, columns], wo[:, part])

        gather(1, m, last, back_out)
        mix_grad[...] = acc[:, :q_width].astype(jnp.bfloat16)
        start_cut(1, m)
        correction = jnp.zeros((rows, 1), jnp.float32)
        for g in range(pairs):
            query, key, value = head_parts(m, g)
            attn = weights[m, g]
            grads = stack(mix_grad[:, g * group * HEAD_DIM:(g + 1) * group * HEAD_DIM])
            value_grad = inner(attn.astype(jnp.bfloat16), grads).astype(jnp.bfloat16)
            weight_grad = outer_side(grads, value)
            score_grad = (
                attn
                * (weight_grad - jnp.sum(weight_grad * attn, -1, keepdims=True))
                * HEAD_DIM ** (-0.5)
            ).astype(jnp.bfloat16)
            query_grad = plain(score_grad, key).astype(jnp.bfloat16)
            key_grad = inner(score_grad, query).astype(jnp.bfloat16)
            query_part = row_dot(query_grad, query)
            correction = correction + row_dot(key_grad, key) + row_dot(value_grad, value)
            for a in range(group):
                correction = correction + query_part[a * rows:(a + 1) * rows]
                at = (g * group + a) * HEAD_DIM
                pair_rows[line, at:at + HEAD_DIM] = query_grad[a * rows:(a + 1) * rows]
            at = q_width + 2 * g * HEAD_DIM
            pair_rows[line, at:at + HEAD_DIM] = key_grad
            pair_rows[line, at + HEAD_DIM:at + 2 * HEAD_DIM] = value_grad

        def back_in(base, start, size):
            part = pl.ds(pl.multiple_of(base + start, size), size)
            return outer_side(pair_rows[line, :q_width], wq[part, :]) + outer_side(
                pair_rows[line, q_width:], wkv[part, :]
            )

        scale = scales[m][:, :1]
        corr_out[m] = jnp.broadcast_to(correction / scale, (rows, HEAD_DIM))
        for distance in range(1, ranks):
            corr_copy(m, distance).start()
        start_rows(1, m)

        for distance in range(1, ranks):
            owner = peer(distance)

            def far(start, size):
                partial = back_in(owner * width, start, size)
                send_b[m, distance - 1, :, pl.ds(start, size)] = partial.astype(jnp.bfloat16)
                sum_copy(1, m, lax.div(start, size), distance).start()

            tiles(width, far)

        total = corr_out[m]
        for distance in range(1, ranks):
            corr_copy(m, distance).wait()
            total = total + corr_in[m, distance - 1]
        factor = scale * scale * scale / model * total[:, :1]

        def near(start, size):
            index, columns = lax.div(start, size), pl.ds(start, size)
            partial = back_in(rank * width, start, size)
            for distance in range(1, ranks):
                sum_copy(1, m, index, distance).wait()
                partial = partial + recv_b[m, distance - 1, :, columns].astype(jnp.float32)
            wide = hfull[m, rank, :, columns].astype(jnp.float32)
            gain = gain_all[rank, :, columns][:1].astype(jnp.float32)

            @pl.when(station > 0)
            def _():
                next_g[m, :, columns] = (
                    gfull[m, rank, :, columns].astype(jnp.float32)
                    + scale * gain * partial
                    - wide * factor
                ).astype(jnp.bfloat16)
                hop_copy(1, m, index).start()

            gain_grad[0, :, columns] += jnp.broadcast_to(
                jnp.sum(partial * wide * scale, 0, keepdims=True), (8, size)
            )

        tiles(width, near)
        pass_rows(0, m)
        pass_rows(1, m)
        return carry

    lax.fori_loop(0, micro, backward, 0)
    for place in range(1, replicas):
        total_copy(place).start()
    for m in range(micro):
        for kind in range(2):
            for place in range(1, replicas):
                cut_copy(kind, m, place).wait()
            for place in range(1, lines):
                line_copy(kind, m, place).wait_send()
            for place in range(lines):
                core_copy(kind, m, place).wait()
    total = gain_grad[0]
    for place in range(1, replicas):
        total_copy(place).wait()
        total = total + gain_grad[place]
    gain_sum[...] = total

    @pl.when(jnp.logical_not(last))
    def _():
        for m in range(micro):
            for index in range(chunks):
                hop_copy(0, m, index).wait_send()

    @pl.when(station > 0)
    def _():
        for m in range(micro):
            for index in range(chunks):
                hop_copy(1, m, index).wait_send()


def layers(hidden_in, mask, gains, query_weight, pair_weight, out_weight, grad_out):
    ranks, sections = lax.axis_size("tensor"), lax.axis_size("section")
    replicas = lax.axis_size("dp")
    micro, rows, width = hidden_in.shape
    model = ranks * width
    q_width, kv_width = query_weight.shape[1], pair_weight.shape[1]
    pairs = kv_width // (2 * HEAD_DIM)
    group = q_width // (HEAD_DIM * pairs)
    half, wide = jnp.bfloat16, jnp.float32
    vmem = pl.BlockSpec(memory_space=pltpu.VMEM)
    anywhere = pl.BlockSpec(memory_space=pl.ANY)
    others, lines, chunks = ranks - 1, replicas // 2, width // tile_of(width)
    return pl.pallas_call(
        functools.partial(kernel, ranks, sections, replicas, micro),
        out_shape=(
            jax.ShapeDtypeStruct((replicas, micro * rows, model // replicas), half),
            jax.ShapeDtypeStruct((replicas, micro * rows, q_width), half),
            jax.ShapeDtypeStruct((replicas, micro * rows, q_width + kv_width), half),
            jax.ShapeDtypeStruct((replicas, micro * rows, model // replicas), half),
            jax.ShapeDtypeStruct((8, width), wide),
        ),
        in_specs=[anywhere, vmem, vmem, anywhere, anywhere, anywhere, anywhere],
        out_specs=(vmem,) * 5,
        scratch_shapes=[
            pltpu.VMEM((micro * rows, model), half),
            pltpu.VMEM((replicas, 8, width), wide),
            pltpu.VMEM((rows, q_width + kv_width), wide),
            pltpu.VMEM((model, q_width), half),
            pltpu.VMEM((model, kv_width), half),
            pltpu.VMEM((q_width, model), half),
            pltpu.VMEM((micro, ranks, rows, width), half),
            pltpu.VMEM((micro, ranks, rows, width), half),
            pltpu.VMEM((ranks, 16, width), half),
            pltpu.VMEM((micro, rows, HEAD_DIM), wide),
            pltpu.VMEM((micro, rows, q_width), half),
            pltpu.VMEM((micro, rows, kv_width), half),
            pltpu.VMEM((micro, pairs, group * rows, rows), wide),
            pltpu.VMEM((rows, q_width), half),
            pltpu.VMEM((micro, others, rows, width), half),
            pltpu.VMEM((micro, others, rows, width), half),
            pltpu.VMEM((micro, others, rows, width), half),
            pltpu.VMEM((micro, others, rows, width), half),
            pltpu.VMEM((micro, rows, width), half),
            pltpu.VMEM((micro, rows, width), half),
            pltpu.VMEM((micro, rows, HEAD_DIM), wide),
            pltpu.VMEM((micro, others, rows, HEAD_DIM), wide),
            pltpu.SemaphoreType.DMA((3 + 2 * micro,)),
            pltpu.SemaphoreType.DMA((2, others)),
            pltpu.SemaphoreType.DMA((2, 2, micro, chunks, others)),
            pltpu.SemaphoreType.DMA((2, 2, micro, chunks, others)),
            pltpu.SemaphoreType.DMA((2, 2, micro, chunks)),
            pltpu.SemaphoreType.DMA((2, micro, others)),
            pltpu.SemaphoreType.DMA((2, 2, micro, replicas - 1)),
            pltpu.SemaphoreType.DMA((2, 2, micro, max(lines - 1, 1))),
            pltpu.SemaphoreType.DMA((2, 2, micro, lines)),
            pltpu.SemaphoreType.DMA((2, replicas - 1)),
        ],
        compiler_params=pltpu.CompilerParams(
            collective_id=0, has_side_effects=True, vmem_limit_bytes=60 << 20
        ),
    )(hidden_in, mask, gains, query_weight, pair_weight, out_weight, grad_out)


def shards(hidden_in, lengths, gains, w_query, w_keyval, w_out, grad_out):
    row_count = hidden_in.shape[1]
    query_weight = w_query[0]
    model_width = query_weight.shape[0]
    pair_count = w_keyval.shape[2]
    pair_weight = w_keyval[0].reshape(model_width, -1)
    position = jnp.arange(row_count)
    causal = position[None, :] <= position[:, None]
    mask = (causal[None] & (position[None, None, :] < lengths[:, None, None])).astype(jnp.float32)
    gain_rows = jnp.broadcast_to(gains, (16, gains.shape[1]))
    *gathered, gain_sum = layers(
        hidden_in, mask, gain_rows, query_weight, pair_weight, w_out[0], grad_out
    )
    normed_rows, mixed_rows, pair_rows, outgrad_rows = [
        block.reshape(-1, block.shape[2]) for block in gathered
    ]
    query_width = query_weight.shape[1]
    query_total = inner(normed_rows, pair_rows[:, :query_width])
    pair_total = inner(normed_rows, pair_rows[:, query_width:])
    output_total = inner(mixed_rows, outgrad_rows)
    gain_width = gain_sum.shape[1] // lax.axis_size("dp")
    gain_total = lax.dynamic_slice_in_dim(gain_sum[0], lax.axis_index("dp") * gain_width, gain_width)
    grad_query = query_total[None]
    grad_keyval = pair_total.reshape(1, pair_total.shape[0], pair_count, 2 * HEAD_DIM)
    grad_outproj = output_total[None]
    grad_gain = gain_total[None]
    return (grad_query, grad_keyval, grad_outproj, grad_gain)


def solution(mesh):
    in_specs = (
        P("dp", None, "tensor"),
        P("dp"),
        P("section", "tensor"),
        P("section", None, "tensor"),
        P("section", None, "tensor", None),
        P("section", "tensor", None),
        P("dp", None, "tensor"),
    )
    out_specs = (
        P("section", "dp", "tensor"),
        P("section", "dp", "tensor", None),
        P("section", "tensor", "dp"),
        P("section", ("tensor", "dp")),
    )
    return jax.shard_map(shards, mesh=mesh, in_specs=in_specs, out_specs=out_specs, check_vma=False)
```

```python
import functools

import jax
import jax.numpy as jnp
from jax import lax
from jax.experimental import pallas as pl
from jax.experimental.pallas import tpu as pltpu
from jax.sharding import PartitionSpec as P

HEAD_DIM = 128


EPS = 1e-05
NEG = -1e30


def inner(former, latter):
    return lax.dot_general(
        former, latter, (((0,), (0,)), ((), ())), preferred_element_type=jnp.float32
    )


def outer_side(former, latter):
    return lax.dot_general(
        former, latter, (((1,), (1,)), ((), ())), preferred_element_type=jnp.float32
    )


def plain(former, latter):
    return jnp.dot(former, latter, preferred_element_type=jnp.float32)


def row_dot(former, latter):
    return jnp.sum(former.astype(jnp.float32) * latter.astype(jnp.float32), -1, keepdims=True)


def tile_of(width):
    return 512 if width % 512 == 0 else 256


def tiles(width, body):
    size = tile_of(width)

    def step(index, carry):
        body(pl.multiple_of(index * size, size), size)
        return carry

    lax.fori_loop(0, width // size, step, 0)


def kernel(
    ranks, sections, replicas, micro,
    hidden, mask, gains, wq_hbm, wkv_hbm, wo_hbm, grad_out,
    normed_all, mixed_all, pair_all, grad_all, gain_sum,
    normed, gain_grad, acc,
    wq, wkv, wo, hfull, gfull, gain_all, scales, queries, keyval, weights, mix_grad,
    send_f, recv_f, send_b, recv_b, next_h, next_g, corr_out, corr_in,
    load_sem, part_sem, gain_sem, ag_sem, rs_sem, z_sem, corr_sem, cut_sem, line_sem, core_sem, sum_sem,
):
    rank = lax.axis_index("tensor")
    station = lax.axis_index("section")
    rows = hidden.shape[1]
    width = hidden.shape[2]
    model = ranks * width
    q_width = wq.shape[1]
    pairs = wkv.shape[1] // (2 * HEAD_DIM)
    group = q_width // (HEAD_DIM * pairs)
    chunk = tile_of(width)
    chunks = width // chunk
    mixed, pair_rows = mixed_all.at[0], pair_all.at[0]
    replica = lax.axis_index("dp")
    lines = replicas // 2
    slots = [(d, c) for c in (0, 1) for d in range(lines)]
    cut = model // replicas
    first, last = station == 0, station == sections - 1

    def peer(distance):
        return lax.rem(rank + distance, ranks)

    def twin(slot):
        line = lax.rem(lax.div(replica, 2) + slot[0], lines)
        core = lax.rem(replica + slot[1], 2)
        return line * 2 + core

    def remote(source, target, sems, device):
        return pltpu.make_async_remote_copy(
            src_ref=source, dst_ref=target, send_sem=sems[0], recv_sem=sems[1],
            device_id=device, device_id_type=pl.DeviceIdType.MESH,
        )

    barrier = pltpu.get_barrier_semaphore()
    for distance in range(1, ranks):
        pl.semaphore_signal(
            barrier, inc=1, device_id={"tensor": peer(distance)},
            device_id_type=pl.DeviceIdType.MESH,
        )

    for slot in slots[1:]:
        pl.semaphore_signal(
            barrier, inc=1, device_id={"dp": twin(slot)},
            device_id_type=pl.DeviceIdType.MESH,
        )

    @pl.when(station > 0)
    def _():
        pl.semaphore_signal(
            barrier, inc=1, device_id={"section": station - 1},
            device_id_type=pl.DeviceIdType.MESH,
        )

    @pl.when(station < sections - 1)
    def _():
        pl.semaphore_signal(
            barrier, inc=1, device_id={"section": station + 1},
            device_id_type=pl.DeviceIdType.MESH,
        )

    def features_of(owner, index):
        return pl.ds(pl.multiple_of(owner * width + index * chunk, chunk), chunk)

    def weight_copies(owner, index):
        part, place = features_of(owner, index), owner * chunks + index
        return [
            pltpu.make_async_copy(source.at[part], target.at[part], part_sem.at[kind, place])
            for kind, (source, target) in enumerate(((wq_hbm, wq), (wkv_hbm, wkv)))
        ]

    out_load = pltpu.make_async_copy(wo_hbm, wo, load_sem.at[2])

    def source_copy(way, m):
        return pltpu.make_async_copy(
            (hidden, grad_out)[way].at[m], (hfull, gfull)[way].at[m, rank],
            load_sem.at[3 + way * micro + m],
        )

    @pl.when(first)
    def _():
        for m in range(micro):
            source_copy(0, m).start()

    @pl.when(last)
    def _():
        for m in range(micro):
            source_copy(1, m).start()

    for distance in range(ranks):
        for index in range(chunks):
            for load in weight_copies(lax.rem(rank - distance + ranks, ranks), index):
                load.start()
    out_load.start()

    ends = jnp.where(first, 0, 1) + jnp.where(last, 0, 1)
    pl.semaphore_wait(barrier, ranks - 1 + replicas - 1 + ends)

    def gain_copy(distance):
        return remote(
            gain_all.at[rank], gain_all.at[rank],
            (gain_sem.at[0, distance - 1], gain_sem.at[1, distance - 1]),
            {"tensor": peer(distance)},
        )

    def columns_of(index):
        return pl.ds(pl.multiple_of(index * chunk, chunk), chunk)

    def gather_copy(way, m, index, distance):
        block = (hfull, gfull)[way].at[m, rank, :, columns_of(index)]
        return remote(
            block, block,
            (ag_sem.at[way, 0, m, index, distance - 1], ag_sem.at[way, 1, m, index, distance - 1]),
            {"tensor": peer(distance)},
        )

    def sum_copy(way, m, index, distance):
        columns = columns_of(index)
        return remote(
            (send_f, send_b)[way].at[m, distance - 1, :, columns],
            (recv_f, recv_b)[way].at[m, distance - 1, :, columns],
            (rs_sem.at[way, 0, m, index, distance - 1], rs_sem.at[way, 1, m, index, distance - 1]),
            {"tensor": peer(distance)},
        )

    def corr_copy(m, distance):
        return remote(
            corr_out.at[m], corr_in.at[m, distance - 1],
            (corr_sem.at[0, m, distance - 1], corr_sem.at[1, m, distance - 1]),
            {"tensor": peer(distance)},
        )

    def hop_copy(way, m, index):
        target = station + 1 if way == 0 else station - 1
        target = lax.rem(target + sections, sections)
        columns = columns_of(index)
        return remote(
            (next_h, next_g)[way].at[m, :, columns],
            (hfull, gfull)[way].at[m, rank, :, columns],
            (z_sem.at[way, 0, m, index], z_sem.at[way, 1, m, index]),
            {"section": target},
        )

    def spread(way, m, index):
        for distance in range(1, ranks):
            gather_copy(way, m, index, distance).start()

    def line_of(m):
        return pl.ds(pl.multiple_of(m * rows, rows), rows)

    def cut_of(kind, m, target):
        if kind == 0:
            return normed.at[line_of(m), pl.ds(pl.multiple_of(target * cut, cut), cut)]
        start = lax.rem(target * cut, width)
        return gfull.at[m, lax.div(target * cut, width), :, pl.ds(pl.multiple_of(start, cut), cut)]

    def cut_copy(kind, m, place):
        target = twin(slots[place])
        return remote(
            cut_of(kind, m, target),
            (normed_all, grad_all)[kind].at[place, line_of(m)],
            (cut_sem.at[kind, 0, m, place - 1], cut_sem.at[kind, 1, m, place - 1]),
            {"dp": target},
        )

    def start_cut(kind, m):
        (normed_all, grad_all)[kind][0, line_of(m)] = cut_of(kind, m, replica)[...]
        for place in range(1, replicas):
            cut_copy(kind, m, place).start()

    def line_copy(kind, m, place):
        whole = (mixed_all, pair_all)[kind]
        return remote(
            whole.at[0, line_of(m)], whole.at[place, line_of(m)],
            (line_sem.at[kind, 0, m, place - 1], line_sem.at[kind, 1, m, place - 1]),
            {"dp": twin((place, 0))},
        )

    def core_copy(kind, m, place):
        whole = (mixed_all, pair_all)[kind]
        return remote(
            whole.at[place, line_of(m)], whole.at[lines + place, line_of(m)],
            (core_sem.at[kind, 0, m, place], core_sem.at[kind, 1, m, place]),
            {"dp": twin((0, 1))},
        )

    def start_rows(kind, m):
        for place in range(1, lines):
            line_copy(kind, m, place).start()
        core_copy(kind, m, 0).start()

    def pass_rows(kind, m):
        for place in range(1, lines):
            line_copy(kind, m, place).wait_recv()
            core_copy(kind, m, place).start()

    def total_copy(place):
        return remote(
            gain_grad.at[0], gain_grad.at[place],
            (sum_sem.at[0, place - 1], sum_sem.at[1, place - 1]),
            {"dp": twin(slots[place])},
        )

    gain_all[rank] = gains[...]
    for distance in range(1, ranks):
        gain_copy(distance).start()

    @pl.when(first)
    def _():
        for m in range(micro):
            source_copy(0, m).wait()
            for index in range(chunks):
                spread(0, m, index)

    @pl.when(last)
    def _():
        for m in range(micro):
            source_copy(1, m).wait()
            for index in range(chunks):
                spread(1, m, index)

    for distance in range(1, ranks):
        gain_copy(distance).wait()

    def gather(way, m, at_source, use):
        def near(index, carry):
            @pl.when(jnp.logical_not(at_source))
            def _():
                hop_copy(way, m, index).wait_recv()
                spread(way, m, index)

            use(rank, index)
            return carry

        acc[...] = jnp.zeros(acc.shape, jnp.float32)
        lax.fori_loop(0, chunks, near, 0)
        for distance in range(1, ranks):
            owner = lax.rem(rank - distance + ranks, ranks)

            def far(index, carry, distance=distance, owner=owner):
                gather_copy(way, m, index, distance).wait()
                use(owner, index)
                return carry

            lax.fori_loop(0, chunks, far, 0)

    def gain_of(owner):
        return gain_all[owner][:1].astype(jnp.float32)

    def stack(block):
        return jnp.concatenate(
            [block[:, a * HEAD_DIM:(a + 1) * HEAD_DIM] for a in range(group)], 0
        )

    def head_parts(m, g):
        query = stack(queries[m, :, g * group * HEAD_DIM:(g + 1) * group * HEAD_DIM])
        key = keyval[m, :, 2 * g * HEAD_DIM:(2 * g + 1) * HEAD_DIM]
        value = keyval[m, :, (2 * g + 1) * HEAD_DIM:(2 * g + 2) * HEAD_DIM]
        return query, key, value

    def forward(m, carry):
        line = line_of(m)

        scales[m] = jnp.zeros((rows, HEAD_DIM), jnp.float32)

        def project(owner, index):
            @pl.when(m == 0)
            def _():
                for load in weight_copies(owner, index):
                    load.wait()

            columns, part = columns_of(index), features_of(owner, index)
            wide = hfull[m, owner, :, columns].astype(jnp.float32)
            scales[m] += jnp.broadcast_to(
                jnp.sum(wide * wide, -1, keepdims=True), (rows, HEAD_DIM)
            )
            gain = gain_all[owner, :, columns][:1].astype(jnp.float32)
            raised = (wide * gain).astype(jnp.bfloat16)
            acc[:, :q_width] += plain(raised, wq[part, :])
            acc[:, q_width:] += plain(raised, wkv[part, :])

        gather(0, m, first, project)
        scale = lax.rsqrt(scales[m][:, :1] / model + EPS)
        scales[m] = jnp.broadcast_to(scale, (rows, HEAD_DIM))
        queries[m] = (acc[:, :q_width] * scale).astype(jnp.bfloat16)
        keyval[m] = (acc[:, q_width:] * scale).astype(jnp.bfloat16)
        allowed = jnp.concatenate([mask[m]] * group, 0) > 0.5
        for g in range(pairs):
            query, key, value = head_parts(m, g)
            scores = outer_side(query, key) * HEAD_DIM ** (-0.5)
            scores = jnp.where(allowed, scores, NEG)
            raised = jnp.exp(scores - jnp.max(scores, -1, keepdims=True))
            attn = raised / jnp.sum(raised, -1, keepdims=True)
            weights[m, g] = attn
            mix = plain(attn.astype(jnp.bfloat16), value).astype(jnp.bfloat16)
            for a in range(group):
                at = (g * group + a) * HEAD_DIM
                mixed[line, at:at + HEAD_DIM] = mix[a * rows:(a + 1) * rows]

        start_rows(0, m)

        @pl.when(m == 0)
        def _():
            out_load.wait()

        @pl.when(jnp.logical_not(last))
        def _():
            for distance in range(1, ranks):
                base = peer(distance) * width

                def project_far(start, size):
                    far = pl.ds(pl.multiple_of(base + start, size), size)
                    send_f[m, distance - 1, :, pl.ds(start, size)] = plain(
                        mixed[line, :], wo[:, far]
                    ).astype(jnp.bfloat16)
                    sum_copy(0, m, lax.div(start, size), distance).start()

                tiles(width, project_far)

            def project_own(start, size):
                near = pl.ds(pl.multiple_of(rank * width + start, size), size)
                index, columns = lax.div(start, size), pl.ds(start, size)
                result = plain(mixed[line, :], wo[:, near])
                for distance in range(1, ranks):
                    sum_copy(0, m, index, distance).wait()
                    result = result + recv_f[m, distance - 1, :, columns].astype(jnp.float32)
                next_h[m, :, columns] = (
                    hfull[m, rank, :, columns].astype(jnp.float32) + result
                ).astype(jnp.bfloat16)
                hop_copy(0, m, index).start()

            tiles(width, project_own)

        for owner in range(ranks):
            wide = hfull[m, owner].astype(jnp.float32)
            normed[line, owner * width:(owner + 1) * width] = (
                wide * scale * gain_of(owner)
            ).astype(jnp.bfloat16)
        start_cut(0, m)
        return carry

    lax.fori_loop(0, micro, forward, 0)
    gain_grad[0] = jnp.zeros(gain_grad.shape[1:], jnp.float32)

    def backward(m, carry):
        line = line_of(m)

        def back_out(owner, index):
            columns, part = columns_of(index), features_of(owner, index)
            acc[:, :q_width] += outer_side(gfull[m, owner, :, columns], wo[:, part])

        gather(1, m, last, back_out)
        mix_grad[...] = acc[:, :q_width].astype(jnp.bfloat16)
        start_cut(1, m)
        correction = jnp.zeros((rows, 1), jnp.float32)
        for g in range(pairs):
            query, key, value = head_parts(m, g)
            attn = weights[m, g]
            grads = stack(mix_grad[:, g * group * HEAD_DIM:(g + 1) * group * HEAD_DIM])
            value_grad = inner(attn.astype(jnp.bfloat16), grads).astype(jnp.bfloat16)
            weight_grad = outer_side(grads, value)
            score_grad = (
                attn
                * (weight_grad - jnp.sum(weight_grad * attn, -1, keepdims=True))
                * HEAD_DIM ** (-0.5)
            ).astype(jnp.bfloat16)
            query_grad = plain(score_grad, key).astype(jnp.bfloat16)
            key_grad = inner(score_grad, query).astype(jnp.bfloat16)
            query_part = row_dot(query_grad, query)
            correction = correction + row_dot(key_grad, key) + row_dot(value_grad, value)
            for a in range(group):
                correction = correction + query_part[a * rows:(a + 1) * rows]
                at = (g * group + a) * HEAD_DIM
                pair_rows[line, at:at + HEAD_DIM] = query_grad[a * rows:(a + 1) * rows]
            at = q_width + 2 * g * HEAD_DIM
            pair_rows[line, at:at + HEAD_DIM] = key_grad
            pair_rows[line, at + HEAD_DIM:at + 2 * HEAD_DIM] = value_grad

        def back_in(base, start, size):
            part = pl.ds(pl.multiple_of(base + start, size), size)
            return outer_side(pair_rows[line, :q_width], wq[part, :]) + outer_side(
                pair_rows[line, q_width:], wkv[part, :]
            )

        scale = scales[m][:, :1]
        corr_out[m] = jnp.broadcast_to(correction / scale, (rows, HEAD_DIM))
        for distance in range(1, ranks):
            corr_copy(m, distance).start()
        start_rows(1, m)

        for distance in range(1, ranks):
            owner = peer(distance)

            def far(start, size):
                partial = back_in(owner * width, start, size)
                send_b[m, distance - 1, :, pl.ds(start, size)] = partial.astype(jnp.bfloat16)
                sum_copy(1, m, lax.div(start, size), distance).start()

            tiles(width, far)

        total = corr_out[m]
        for distance in range(1, ranks):
            corr_copy(m, distance).wait()
            total = total + corr_in[m, distance - 1]
        factor = scale * scale * scale / model * total[:, :1]

        def near(start, size):
            index, columns = lax.div(start, size), pl.ds(start, size)
            partial = back_in(rank * width, start, size)
            for distance in range(1, ranks):
                sum_copy(1, m, index, distance).wait()
                partial = partial + recv_b[m, distance - 1, :, columns].astype(jnp.float32)
            wide = hfull[m, rank, :, columns].astype(jnp.float32)
            gain = gain_all[rank, :, columns][:1].astype(jnp.float32)

            @pl.when(station > 0)
            def _():
                next_g[m, :, columns] = (
                    gfull[m, rank, :, columns].astype(jnp.float32)
                    + scale * gain * partial
                    - wide * factor
                ).astype(jnp.bfloat16)
                hop_copy(1, m, index).start()

            gain_grad[0, :, columns] += jnp.broadcast_to(
                jnp.sum(partial * wide * scale, 0, keepdims=True), (8, size)
            )

        tiles(width, near)
        pass_rows(0, m)
        pass_rows(1, m)
        return carry

    lax.fori_loop(0, micro, backward, 0)
    for place in range(1, replicas):
        total_copy(place).start()
    for m in range(micro):
        for kind in range(2):
            for place in range(1, replicas):
                cut_copy(kind, m, place).wait()
            for place in range(1, lines):
                line_copy(kind, m, place).wait_send()
            for place in range(lines):
                core_copy(kind, m, place).wait()
    total = gain_grad[0]
    for place in range(1, replicas):
        total_copy(place).wait()
        total = total + gain_grad[place]
    gain_sum[...] = total

    @pl.when(jnp.logical_not(last))
    def _():
        for m in range(micro):
            for index in range(chunks):
                hop_copy(0, m, index).wait_send()

    @pl.when(station > 0)
    def _():
        for m in range(micro):
            for index in range(chunks):
                hop_copy(1, m, index).wait_send()


def layers(hidden_in, mask, gains, query_weight, pair_weight, out_weight, grad_out):
    ranks, sections = lax.axis_size("tensor"), lax.axis_size("section")
    replicas = lax.axis_size("dp")
    micro, rows, width = hidden_in.shape
    model = ranks * width
    q_width, kv_width = query_weight.shape[1], pair_weight.shape[1]
    pairs = kv_width // (2 * HEAD_DIM)
    group = q_width // (HEAD_DIM * pairs)
    half, wide = jnp.bfloat16, jnp.float32
    vmem = pl.BlockSpec(memory_space=pltpu.VMEM)
    anywhere = pl.BlockSpec(memory_space=pl.ANY)
    others, lines, chunks = ranks - 1, replicas // 2, width // tile_of(width)
    return pl.pallas_call(
        functools.partial(kernel, ranks, sections, replicas, micro),
        out_shape=(
            jax.ShapeDtypeStruct((replicas, micro * rows, model // replicas), half),
            jax.ShapeDtypeStruct((replicas, micro * rows, q_width), half),
            jax.ShapeDtypeStruct((replicas, micro * rows, q_width + kv_width), half),
            jax.ShapeDtypeStruct((replicas, micro * rows, model // replicas), half),
            jax.ShapeDtypeStruct((8, width), wide),
        ),
        in_specs=[anywhere, vmem, vmem, anywhere, anywhere, anywhere, anywhere],
        out_specs=(vmem,) * 5,
        scratch_shapes=[
            pltpu.VMEM((micro * rows, model), half),
            pltpu.VMEM((replicas, 8, width), wide),
            pltpu.VMEM((rows, q_width + kv_width), wide),
            pltpu.VMEM((model, q_width), half),
            pltpu.VMEM((model, kv_width), half),
            pltpu.VMEM((q_width, model), half),
            pltpu.VMEM((micro, ranks, rows, width), half),
            pltpu.VMEM((micro, ranks, rows, width), half),
            pltpu.VMEM((ranks, 16, width), half),
            pltpu.VMEM((micro, rows, HEAD_DIM), wide),
            pltpu.VMEM((micro, rows, q_width), half),
            pltpu.VMEM((micro, rows, kv_width), half),
            pltpu.VMEM((micro, pairs, group * rows, rows), wide),
            pltpu.VMEM((rows, q_width), half),
            pltpu.VMEM((micro, others, rows, width), half),
            pltpu.VMEM((micro, others, rows, width), half),
            pltpu.VMEM((micro, others, rows, width), half),
            pltpu.VMEM((micro, others, rows, width), half),
            pltpu.VMEM((micro, rows, width), half),
            pltpu.VMEM((micro, rows, width), half),
            pltpu.VMEM((micro, rows, HEAD_DIM), wide),
            pltpu.VMEM((micro, others, rows, HEAD_DIM), wide),
            pltpu.SemaphoreType.DMA((3 + 2 * micro,)),
            pltpu.SemaphoreType.DMA((2, ranks * chunks)),
            pltpu.SemaphoreType.DMA((2, others)),
            pltpu.SemaphoreType.DMA((2, 2, micro, chunks, others)),
            pltpu.SemaphoreType.DMA((2, 2, micro, chunks, others)),
            pltpu.SemaphoreType.DMA((2, 2, micro, chunks)),
            pltpu.SemaphoreType.DMA((2, micro, others)),
            pltpu.SemaphoreType.DMA((2, 2, micro, replicas - 1)),
            pltpu.SemaphoreType.DMA((2, 2, micro, max(lines - 1, 1))),
            pltpu.SemaphoreType.DMA((2, 2, micro, lines)),
            pltpu.SemaphoreType.DMA((2, replicas - 1)),
        ],
        compiler_params=pltpu.CompilerParams(
            collective_id=0, has_side_effects=True, vmem_limit_bytes=60 << 20
        ),
    )(hidden_in, mask, gains, query_weight, pair_weight, out_weight, grad_out)


def shards(hidden_in, lengths, gains, w_query, w_keyval, w_out, grad_out):
    row_count = hidden_in.shape[1]
    query_weight = w_query[0]
    model_width = query_weight.shape[0]
    pair_count = w_keyval.shape[2]
    pair_weight = w_keyval[0].reshape(model_width, -1)
    position = jnp.arange(row_count)
    causal = position[None, :] <= position[:, None]
    mask = (causal[None] & (position[None, None, :] < lengths[:, None, None])).astype(jnp.float32)
    gain_rows = jnp.broadcast_to(gains, (16, gains.shape[1]))
    *gathered, gain_sum = layers(
        hidden_in, mask, gain_rows, query_weight, pair_weight, w_out[0], grad_out
    )
    normed_rows, mixed_rows, pair_rows, outgrad_rows = [
        block.reshape(-1, block.shape[2]) for block in gathered
    ]
    query_width = query_weight.shape[1]
    query_total = inner(normed_rows, pair_rows[:, :query_width])
    pair_total = inner(normed_rows, pair_rows[:, query_width:])
    output_total = inner(mixed_rows, outgrad_rows)
    gain_width = gain_sum.shape[1] // lax.axis_size("dp")
    gain_total = lax.dynamic_slice_in_dim(gain_sum[0], lax.axis_index("dp") * gain_width, gain_width)
    grad_query = query_total[None]
    grad_keyval = pair_total.reshape(1, pair_total.shape[0], pair_count, 2 * HEAD_DIM)
    grad_outproj = output_total[None]
    grad_gain = gain_total[None]
    return (grad_query, grad_keyval, grad_outproj, grad_gain)


def solution(mesh):
    in_specs = (
        P("dp", None, "tensor"),
        P("dp"),
        P("section", "tensor"),
        P("section", None, "tensor"),
        P("section", None, "tensor", None),
        P("section", "tensor", None),
        P("dp", None, "tensor"),
    )
    out_specs = (
        P("section", "dp", "tensor"),
        P("section", "dp", "tensor", None),
        P("section", "tensor", "dp"),
        P("section", ("tensor", "dp")),
    )
    return jax.shard_map(shards, mesh=mesh, in_specs=in_specs, out_specs=out_specs, check_vma=False)
```
